32 devices in a mesh: groups: 1, dp: 16 (over z, x, core), heads: 2 (over y).
Axes of the slice: x: 2, y: 2, z: 4, core: 2. Of those that a mesh axis runs over, the one named last changes fastest.
Arguments:
- queries: bfloat16 [256, 128, 576], P(('groups', 'dp'), 'heads'), may hold values from -21 to 21
- kv_cache: bfloat16 [256, 256, 576], P(('groups', 'dp')), may hold values from -4 to 4
- lengths: int32 [256], P(('groups', 'dp')), may hold values from 1 to 256, as said below
- resid: bfloat16 [256, 7168], P(('groups', 'dp')), may hold values from -6 to 6
- w_uv: bfloat16 [2, 64, 512, 128], P('heads', 'dp'), may hold values from -0.25 to 0.25
- o_proj: bfloat16 [2, 64, 128, 7168], P('heads', 'dp'), may hold values from -0.046875 to 0.046875
- norm_gain: bfloat16 [7168], replicated, may hold values from 0.25 to 1.75
- expert_ids: int32 [256, 8], P(('groups', 'dp')), may hold values from 0 to 15, all different within a row; in each aligned block of 16 rows (0 to 15, 16 to 31, ...) at most 12 rows name the same one
- route_gates: float32 [256, 8], P(('groups', 'dp')), may hold values from 0.1 to 1
- expert_owner: int32 [16], replicated, may hold values from 0 to 15, each once
- gate_w: bfloat16 [16, 7168, 1024], P('dp', None, 'heads'), may hold values from -0.0625 to 0.0625
- up_w: bfloat16 [16, 7168, 1024], P('dp', None, 'heads'), may hold values from -0.0625 to 0.0625
- down_w: bfloat16 [16, 1024, 7168], P('dp', 'heads'), may hold values from -0.1875 to 0.1875
Outputs:
- layer_out: bfloat16 [256, 7168], P(('groups', 'dp'), 'heads')
The draws below stay inside these ranges and needn't reach their ends.
Inputs may be any that keep to these rules, and one draw needn't show every extreme that they name: `expert_ids`: each row names 8 different experts. Among the rows of one index of dp no expert is named by more than 12 rows, a bound that some block reaches of them. `lengths`: row 0 uses the whole cache.
All inputs are finite; a program needn't handle non-finite values.
Results may differ from the reference program's by a relative error of at most 0.0058.
Values may be sent and summed in bfloat16 or wider, within the bound.
No kernel may reach another device: no remote copies, remote signals or barrier semaphores. Data moves between devices by JAX's collectives and lax.ppermute only.
A program may use at most 128 MiB of HBM per device.

```python
import math
import jax
import jax.numpy as jnp
import numpy as np
from jax import lax

D = 7168
HEADS = 128
LAT = 512
ROPE = 64
VD = 128
FF = 1024
ROWS_DEV = 16
CTX = 256
ROWS = 256
HEADS_SHARD = 64
EXPERTS = 16
TOP = 8
CAP = 12
N_HEADS = 2


def draw_kv_cache(key, part):
    key = jax.random.fold_in(key, 11)
    return jnp.clip(jax.random.normal(key, (ROWS, CTX, LAT + ROPE), jnp.float32), -4.0, 4.0).astype(jnp.bfloat16)


def draw_queries(key, part):
    key = jax.random.fold_in(key, 23)
    drawn_key = jax.random.fold_in(key, 0)
    return jnp.clip(jax.random.normal(drawn_key, (ROWS, HEADS, LAT + ROPE), jnp.float32), -4.0, 4.0).astype(jnp.bfloat16)


def draw_lengths(key, part):
    key = jax.random.fold_in(key, 31)
    first_key, second_key = jax.random.split(key, 2)
    first_len = jax.random.randint(first_key, (ROWS,), 1, CTX + 1)
    second_len = jax.random.randint(second_key, (ROWS,), 1, CTX + 1)
    length_all = jnp.maximum(first_len * second_len // CTX, 1)
    return length_all.at[0].set(CTX).astype(jnp.int32)


def block_levels(key, dims, shards, smallest, largest):
    factor_of, own = 1.0, jax.random.fold_in(key, 6)
    for axis_at, blocks in shards:
        steps = jnp.exp(jax.random.uniform(jax.random.fold_in(own, axis_at), (blocks,), jnp.float32, smallest / len(shards), largest / len(shards)))
        factor_of = factor_of * jnp.repeat(steps, dims[axis_at] // blocks).reshape([-1 if axis == axis_at else 1 for axis in range(len(dims))])
    return factor_of


def assign_block(key, own, number, rows, count, top, most, skew):
    ranking = jax.random.permutation(key, count)
    heavy_load, usual = shares(count, rows * top, most, skew, True), shares(count, rows * top, most, skew, False)
    places = jnp.arange(count)

    def named(tallies, rotation):
        used = int((tallies > 0).sum())
        fixed = max(1, used // 4)
        shifted = fixed + (places - fixed + rotation * (used - fixed)) % max(1, count - fixed)
        return jnp.zeros((count,), jnp.int32).at[ranking[jnp.where(places < fixed, places, shifted)]].set(jnp.asarray(tallies, jnp.int32))

    tallies = jnp.where(number % 4 == 0, named(heavy_load, number // 4), named(usual, number - number // 4 - 1))
    mixed = jax.random.permutation(jax.random.fold_in(own, 3), count)
    donor, receiver = mixed[0:count // 2 * 2:2], mixed[1:count // 2 * 2:2]
    room = jnp.minimum(tallies[donor] - 1, most - tallies[receiver]) // 2
    room = jnp.where((donor == ranking[0]) | (receiver == ranking[0]) | (tallies[receiver] == 0), 0, jnp.maximum(room, 0))
    shifted = jax.random.randint(jax.random.fold_in(own, 4), (count // 2,), 0, 1 << 20) % (room + 1)
    tallies = tallies.at[donor].add(-shifted).at[receiver].add(shifted)
    members = jnp.searchsorted(jnp.cumsum(tallies), jnp.arange(rows * top), side="right").astype(jnp.int32)
    table = members.reshape(top, rows).T
    table = table[jax.random.permutation(jax.random.fold_in(own, 1), rows)]
    rotation = jax.random.randint(jax.random.fold_in(own, 2), (rows, 1), 0, top)
    return jnp.take_along_axis(table, (jnp.arange(top)[None, :] + rotation) % top, axis=1)


def shares(count, total, limit, lean, full):
    loads = [(1 << 20) // math.isqrt(grade ** lean) + 1 for grade in range(1, count + 1)]
    largest = limit if full else min(limit, max(-(-total // count), total * loads[0] // sum(loads)))
    least = 1 if total - largest >= count - 1 else 0
    holding, spare = [largest] + [least] * (count - 1), total - largest - least * (count - 1)
    while spare > 0:
        candidates = [i for i in range(1, count) if holding[i] < largest] or [i for i in range(1, count) if holding[i] < limit]
        mass, remaining = sum([loads[i] for i in candidates]), spare
        for i in candidates:
            more = min(limit - holding[i], max(1, remaining * loads[i] // mass), spare)
            holding[i] = holding[i] + more
            spare = spare - more
    return np.array(holding)


def gaussian(key, extent, deviation, limit, cuts=(), held_as=jnp.bfloat16):
    array = jax.random.normal(key, extent, jnp.float32) * deviation
    if len(cuts) > 0:
        array = block_levels(key, extent, cuts, -0.22, 0.18) * array
    return jnp.clip(array, min=-limit, max=limit).astype(held_as)


def setup_inputs(seed: int = 0, part: int = 0) -> dict:
    arg_keys = jax.random.split(jax.random.key(seed), 14)
    part_keys = jax.random.split(jax.random.fold_in(arg_keys[13], part), 14)
    queries = draw_queries(jax.random.fold_in(jax.random.fold_in(arg_keys[13], part), 71), part)
    kv_cache = draw_kv_cache(jax.random.fold_in(jax.random.fold_in(arg_keys[13], part), 71), part)
    lengths = draw_lengths(jax.random.fold_in(jax.random.fold_in(arg_keys[13], part), 71), part)
    resid = gaussian(part_keys[3], (ROWS, D), 1.0, 6.0, ((0, 16),))
    w_uv = gaussian(arg_keys[4], (N_HEADS, HEADS_SHARD, LAT, VD), LAT ** -0.5, 0.25, ((0, 2), (1, 16)))
    o_proj = gaussian(arg_keys[5], (N_HEADS, HEADS_SHARD, VD, D), (HEADS * VD) ** -0.5, 0.046875, ((0, 2), (1, 16)))
    norm_gain = jnp.clip(1.0 + 0.15 * jax.random.normal(arg_keys[6], (D,), jnp.float32), 0.25, 1.75).astype(jnp.bfloat16)
    expert_ids_keys = jax.random.split(jax.random.fold_in(part_keys[7], 1), ROWS // ROWS_DEV)
    expert_ids_turns = jax.random.permutation(jax.random.fold_in(part_keys[7], 3), ROWS // ROWS_DEV)
    expert_ids = jax.vmap(lambda own, number: assign_block(jax.random.fold_in(part_keys[7], 2), own, number, ROWS_DEV, EXPERTS, TOP, CAP, 2))(expert_ids_keys, expert_ids_turns).reshape((ROWS, TOP))
    route_gates = jnp.clip(0.1 + 0.9 * jax.random.uniform(part_keys[8], (ROWS, TOP), jnp.float32) ** block_levels(part_keys[8], (ROWS, TOP), ((0, 16),), -0.2, 0.2), 0.1, 1.0)
    expert_owner = jax.random.permutation(arg_keys[9], EXPERTS).astype(jnp.int32)
    gate_w = gaussian(arg_keys[10], (EXPERTS, D, FF), D ** -0.5, 0.0625, ((0, 16), (2, 2)))
    up_w = gaussian(arg_keys[11], (EXPERTS, D, FF), D ** -0.5, 0.0625, ((0, 16), (2, 2)))
    down_w = gaussian(arg_keys[12], (EXPERTS, FF, D), FF ** -0.5, 0.1875, ((0, 16), (1, 2)))
    return {"queries": queries, "kv_cache": kv_cache, "lengths": lengths, "resid": resid, "w_uv": w_uv, "o_proj": o_proj, "norm_gain": norm_gain, "expert_ids": expert_ids, "route_gates": route_gates, "expert_owner": expert_owner, "gate_w": gate_w, "up_w": up_w, "down_w": down_w}


EPSILON = 1e-06
SCORE_SCALE = 192.0 ** (-0.5)

def attend(queries, kv_cache, lengths):
    scores = jnp.einsum('rhk,rck->rhc', queries.astype(jnp.float32), kv_cache.astype(jnp.float32)) * SCORE_SCALE
    positions = lax.broadcasted_iota(jnp.int32, (1, 1, kv_cache.shape[1]), 2)
    visible = positions < lengths.astype(jnp.int32)[:, None, None]
    scores = jnp.where(visible, scores, -jnp.inf)
    peak = lax.optimization_barrier(jnp.max(scores, -1, keepdims=True))
    weights = jnp.exp(scores - peak)
    weights = (weights / lax.optimization_barrier(jnp.sum(weights, -1, keepdims=True))).astype(jnp.bfloat16)
    latent = kv_cache[:, :, :LAT]
    mixed = jnp.einsum('rhc,rcl->rhl', weights.astype(jnp.float32), latent.astype(jnp.float32))
    return mixed.astype(jnp.bfloat16)

def reference(queries, kv_cache, lengths, resid, w_uv, o_proj, norm_gain, expert_ids, route_gates, expert_owner, gate_w, up_w, down_w):
    latent_out = attend(queries, kv_cache, lengths)
    value_maps = w_uv.reshape(HEADS, LAT, VD)
    values = jnp.einsum('rhl,hlv->rhv', latent_out.astype(jnp.float32), value_maps.astype(jnp.float32)).astype(jnp.bfloat16)
    attention = jnp.dot(values.reshape(ROWS, HEADS * VD), o_proj.reshape(HEADS * VD, D), preferred_element_type=jnp.float32)
    mid = resid.astype(jnp.float32) + attention
    mean_square = lax.optimization_barrier(jnp.mean(mid * mid, -1, keepdims=True))
    normed = (mid * lax.rsqrt(mean_square + EPSILON) * norm_gain.astype(jnp.float32)).astype(jnp.bfloat16)
    matches = expert_ids[:, :, None] == jnp.arange(EXPERTS, dtype=jnp.int32)[None, None, :]
    weights_mix = lax.optimization_barrier(jnp.sum(jnp.where(matches, route_gates[:, :, None], jnp.float32(0.0)), 1))

    def accumulate(running, expert):
        holder = expert_owner[expert]
        gate_act = jnp.dot(normed, gate_w[holder], preferred_element_type=jnp.float32)
        up_act = jnp.dot(normed, up_w[holder], preferred_element_type=jnp.float32)
        hidden_units = (jax.nn.silu(gate_act) * up_act).astype(jnp.bfloat16)
        expert_out = jnp.dot(hidden_units, down_w[holder], preferred_element_type=jnp.float32)
        column = lax.dynamic_slice_in_dim(weights_mix, expert, 1, 1)
        return (running + column * expert_out, None)
    routed, _ = lax.scan(accumulate, jnp.zeros((ROWS, D), jnp.float32), jnp.arange(EXPERTS, dtype=jnp.int32))
    return (mid + routed).astype(jnp.bfloat16)
```

```python
import functools

import jax
import jax.numpy as jnp
from jax import lax
from jax.experimental import pallas as pl
from jax.experimental.pallas import tpu as pltpu
from jax.sharding import PartitionSpec as P

LAT = 512
EPSILON = 1e-06
SCORE_SCALE = 192.0 ** (-0.5)
BF16 = jnp.bfloat16
F32 = jnp.float32
EXTRA = 128
VMEM_BYTES = 56 * 1024 * 1024


def attend(queries, kv_cache, lengths):
    scores = (
        jnp.einsum("rhk,rck->rhc", queries, kv_cache, preferred_element_type=F32) * SCORE_SCALE
    )
    positions = lax.broadcasted_iota(jnp.int32, (1, 1, kv_cache.shape[1]), 2)
    visible = positions < lengths[:, None, None]
    scores = jnp.where(visible, scores, -jnp.inf)
    peak = jnp.max(scores, -1, keepdims=True)
    weights = jnp.exp(scores - peak)
    weights = (weights / jnp.sum(weights, -1, keepdims=True)).astype(BF16)
    latent = kv_cache[:, :, :LAT]
    mixed = jnp.einsum("rhc,rcl->rhl", weights, latent, preferred_element_type=F32)
    return mixed.astype(BF16)


class Net:
    def __init__(self, dp, heads):
        self.dp, self.heads = dp, heads
        self.near = 2
        self.line = dp // 4
        self.plane = [(jh, jx) for jh in range(heads) for jx in range(self.near)]

    def move(self, value, dp_mask, heads_mask=0):
        mask = dp_mask * self.heads + heads_mask
        count = self.dp * self.heads
        return lax.ppermute(value, ("dp", "heads"), [(i, i ^ mask) for i in range(count)])

    def core(self, value):
        return self.move(value, 1)

    def in_plane(self, value, at):
        jh, jx = self.plane[at]
        return self.move(value, 2 * jx, jh)

    def in_line(self, value, jz):
        return self.move(value, 4 * jz)


def project_kernel(order, cols, x_ref, scale_ref, w_ref, keep_ref, send_ref, x_scr, *, block, scaled):
    @pl.when((pl.program_id(0) == 0) & (pl.program_id(1) == 0))
    def _():
        for slot in range(x_ref.shape[0] // block):
            start = pl.multiple_of(order[slot] * block, block)
            x_scr[slot * block : (slot + 1) * block, :] = x_ref[pl.ds(start, block), :]

    half = x_ref.shape[0] // 2
    out = jnp.dot(x_scr[...], w_ref[...], preferred_element_type=F32)
    if scaled:
        out = out * scale_ref[:, :1]
    keep_ref[0] = out[:half].astype(BF16)
    send_ref[0] = out[half:].astype(BF16)


def project(x, weights, order, cols, scale, tile, first, count, block):
    rows, depth = x.shape
    heads = cols.shape[0]
    per_slice = weights.shape[1] // (tile * heads)
    out = jax.ShapeDtypeStruct((heads, rows // 2, count * tile), BF16)
    scaled = scale is not None
    if scale is None:
        scale = jnp.zeros((8, EXTRA), F32)
    spec = pl.BlockSpec((1, rows // 2, tile), lambda h, t, o, c: (h, 0, t))
    return pl.pallas_call(
        functools.partial(project_kernel, block=block, scaled=scaled),
        grid_spec=pltpu.PrefetchScalarGridSpec(
            num_scalar_prefetch=2,
            grid=(heads, count),
            in_specs=[
                pl.BlockSpec((rows, depth), lambda h, t, o, c: (0, 0)),
                pl.BlockSpec(scale.shape, lambda h, t, o, c: (0, 0)),
                pl.BlockSpec((depth, tile), lambda h, t, o, c: (0, c[h] * per_slice + first + t)),
            ],
            out_specs=[spec, spec],
            scratch_shapes=[pltpu.VMEM((rows, depth), BF16)],
        ),
        out_shape=[out, out],
        compiler_params=pltpu.CompilerParams(vmem_limit_bytes=VMEM_BYTES),
        cost_estimate=pl.CostEstimate(
            flops=2 * rows * depth * count * tile * heads,
            bytes_accessed=2 * (depth + rows) * count * tile * heads,
            transcendentals=0,
        ),
    )(order, cols, x, scale, weights)


def pieces_of(value):
    high = lax.reduce_precision(value, 8, 7)
    rest = value - high
    middle = lax.reduce_precision(rest, 8, 7)
    return [high.astype(BF16), middle.astype(BF16), (rest - middle).astype(BF16)]


def row_parts(pieces, jh, net, by_line, rows_dev, lanes):
    parts = []
    for jc in range(2):
        for jx in range(net.near):
            at = jh * net.near + jx
            if by_line:
                for jz in range(net.line):
                    ref = pieces[jc][jz]
                    parts.append(ref[at * rows_dev : (at + 1) * rows_dev, lanes])
            else:
                parts.append(pieces[jc][at][:, lanes])
    return jnp.concatenate(parts, 0)


def gate_up_kernel(cols, me, *refs, net, by_line, rows_dev, tile, count, last, width):
    per_core = net.line if by_line else len(net.plane)
    pieces = [refs[:per_core], refs[per_core : 2 * per_core]]
    refs = refs[2 * per_core :]
    gate_ref, up_ref = refs[:2]
    refs = refs[2:]
    jh = pl.program_id(0)
    step = pl.program_id(1)
    if last:
        gate_in, up_in, squares_in, hidden_ref, coef_ref, gate_acc, up_acc = refs
    else:
        gate_acc, up_acc, squares_ref = refs

    @pl.when((jh == 0) & (step == 0))
    def _():
        if last:
            gate_acc[...] = gate_in[...]
            up_acc[...] = up_in[...]
        else:
            gate_acc[...] = jnp.zeros_like(gate_acc)
            up_acc[...] = jnp.zeros_like(up_acc)

    for which in range(net.heads):

        @pl.when(jh == which)
        def _():
            lanes = pl.ds(pl.multiple_of(step * tile, tile), tile)
            x = row_parts(pieces, which, net, by_line, rows_dev, lanes)
            gate_acc[...] += jnp.dot(x, gate_ref[...], preferred_element_type=F32)
            up_acc[...] += jnp.dot(x, up_ref[...], preferred_element_type=F32)

    @pl.when((jh == net.heads - 1) & (step == count - 1))
    def _():
        lanes = pl.ds(count * tile, EXTRA)
        extras = [
            row_parts(pieces, h, net, by_line, rows_dev, lanes).astype(F32)
            for h in range(net.heads)
        ]
        lane = lax.broadcasted_iota(jnp.int32, (1, EXTRA), 1)
        squares = sum(extras)
        squares = jnp.sum(jnp.where(lane < 3, squares, 0.0), -1, keepdims=True)
        if not last:
            squares_ref[...] = jnp.broadcast_to(squares, squares_ref.shape)
        else:
            total = squares + squares_in[:, :1]
            norm = lax.rsqrt(total / width + EPSILON)
            mine = (lane == 3 + me[0]) | (lane == 3 + net.dp + me[0]) | (lane == 3 + 2 * net.dp + me[0])
            coef = jnp.sum(jnp.where(mine, extras[0], 0.0), -1, keepdims=True)
            coef_ref[...] = jnp.broadcast_to(coef, coef_ref.shape)
            gate = gate_acc[...] * norm
            up = up_acc[...] * norm
            hidden_ref[...] = (gate / (1.0 + jnp.exp(-gate)) * up).astype(BF16)


def gate_up(net, pieces, by_line, gate_w, up_w, cols, me, tile, first, count, rows_dev, before=None):
    flat = [piece for group in pieces for piece in group]
    width, hidden = gate_w.shape
    rows = net.dp * rows_dev
    per_slice = width // (tile * net.heads)
    last = before is not None
    weight = pl.BlockSpec((tile, hidden), lambda h, t, c, m: (c[h] * per_slice + first + t, 0))
    whole = lambda shape: pl.BlockSpec(shape, lambda h, t, c, m: (0,) * len(shape))
    in_specs = [whole(piece.shape) for piece in flat] + [weight, weight]
    operands = [cols, me, *flat, gate_w, up_w]
    acc = jax.ShapeDtypeStruct((rows, hidden), F32)
    wide = jax.ShapeDtypeStruct((rows, EXTRA), F32)
    if last:
        in_specs += [whole(value.shape) for value in before]
        operands += list(before)
        outs = [jax.ShapeDtypeStruct((rows, hidden), BF16), wide]
        scratch = [pltpu.VMEM(acc.shape, F32), pltpu.VMEM(acc.shape, F32)]
    else:
        outs = [acc, acc, wide]
        scratch = []
    return pl.pallas_call(
        functools.partial(
            gate_up_kernel,
            net=net,
            by_line=by_line,
            rows_dev=rows_dev,
            tile=tile,
            count=count,
            last=last,
            width=width,
        ),
        grid_spec=pltpu.PrefetchScalarGridSpec(
            num_scalar_prefetch=2,
            grid=(net.heads, count),
            in_specs=in_specs,
            out_specs=[whole(out.shape) for out in outs],
            scratch_shapes=scratch,
        ),
        out_shape=outs,
        compiler_params=pltpu.CompilerParams(vmem_limit_bytes=VMEM_BYTES),
        cost_estimate=pl.CostEstimate(
            flops=4 * rows * count * tile * net.heads * hidden,
            bytes_accessed=4 * count * tile * net.heads * hidden,
            transcendentals=0,
        ),
    )(*operands)


def add_up(keep, received, pick):
    total = pick(keep).astype(F32)
    for value in received:
        total = total + value.astype(F32)
    return total


def reduce_plane_first(net, keep, send, rows_dev):
    other = net.core(send)
    width = keep.shape[-1]
    shape = (len(net.plane), net.line * rows_dev, width)
    keep, other = keep.reshape(shape), other.reshape(shape)
    summed = [keep[at].astype(F32) + other[at].astype(F32) for at in range(len(net.plane))]
    total = summed[0]
    arrived = [net.in_plane(summed[at].astype(BF16), at) for at in range(1, len(net.plane))]
    for value in arrived:
        total = total + value.astype(F32)
    total = total.reshape(net.line, rows_dev, width)
    arrived = [net.in_line(total[jz].astype(BF16), jz) for jz in range(1, net.line)]
    out = total[0]
    for value in arrived:
        out = out + value.astype(F32)
    return out


def reduce_line_first(net, keep, send, rows_dev):
    other = net.core(send)
    width = keep.shape[-1]
    shape = (len(net.plane), net.line, rows_dev, width)
    keep, other = keep.reshape(shape), other.reshape(shape)
    summed = [keep[:, jz].astype(F32) + other[:, jz].astype(F32) for jz in range(net.line)]
    total = summed[0]
    arrived = [net.in_line(summed[jz].astype(BF16), jz) for jz in range(1, net.line)]
    for value in arrived:
        total = total + value.astype(F32)
    arrived = [net.in_plane(total[at].astype(BF16), at) for at in range(1, len(net.plane))]
    out = total[0]
    for value in arrived:
        out = out + value.astype(F32)
    return out


def gather_line_first(net, value):
    held = jnp.concatenate([value] + [net.in_line(value, jz) for jz in range(1, net.line)], 0)
    own = [held] + [net.in_plane(held, at) for at in range(1, len(net.plane))]
    return [own, [net.core(piece) for piece in own]]


def gather_plane_first(net, value):
    held = jnp.concatenate([value] + [net.in_plane(value, at) for at in range(1, len(net.plane))], 0)
    own = [held] + [net.in_line(held, jz) for jz in range(1, net.line)]
    return [own, [net.core(piece) for piece in own]]


def on_device(
    queries,
    kv_cache,
    lengths,
    resid,
    w_uv,
    o_proj,
    norm_gain,
    expert_ids,
    route_gates,
    expert_owner,
    gate_w,
    up_w,
    down_w,
):
    dp = lax.axis_size("dp")
    heads = lax.axis_size("heads")
    net = Net(dp, heads)
    rows_dev, width = resid.shape
    slice_width = width // heads
    tile = slice_width // 7
    wide_count, narrow_count = 5, 2
    wide = wide_count * tile
    me = lax.axis_index("dp")
    my_head = lax.axis_index("heads")
    slots = jnp.array(
        [
            jc + 2 * jx + 4 * jz
            for jc in range(2)
            for jx in range(net.near)
            for jz in range(net.line)
        ],
        jnp.int32,
    )
    order = jnp.bitwise_xor(slots, me)
    natural = jnp.arange(dp, dtype=jnp.int32)
    cols = jnp.bitwise_xor(jnp.arange(heads, dtype=jnp.int32), my_head)

    latent_out = attend(queries, kv_cache, lengths)
    gathered = lax.all_to_all(latent_out, "dp", split_axis=1, concat_axis=0, tiled=True)
    values = jnp.einsum("rhl,hlv->rhv", gathered, w_uv[0], preferred_element_type=F32).astype(BF16)
    values = values.reshape(values.shape[0], -1)
    out_proj = o_proj[0].reshape(-1, width)

    holder = jnp.sum(
        (expert_ids[:, :, None] == jnp.arange(expert_owner.shape[0], dtype=jnp.int32)).astype(jnp.int32)
        * expert_owner,
        -1,
    )
    table = jnp.sum(jnp.where(holder[:, :, None] == natural, route_gates[:, :, None], 0.0), 1)
    table_parts = pieces_of(table)

    resid_slice = lax.dynamic_slice_in_dim(resid, my_head * slice_width, slice_width, 1).astype(F32)
    gain_slice = lax.dynamic_slice_in_dim(norm_gain, my_head * slice_width, slice_width, 0).astype(F32)

    def payload(attention, lo, hi):
        mid = resid_slice[:, lo:hi] + attention
        squares = jnp.sum(mid * mid, -1, keepdims=True)
        extra = pieces_of(squares) + table_parts
        pad = jnp.zeros((rows_dev, EXTRA - 3 - 3 * dp), BF16)
        row = (mid * gain_slice[lo:hi]).astype(BF16)
        return mid, jnp.concatenate([row, *extra, pad], 1)

    keep_a, send_a = project(values, out_proj, order, cols, None, tile, 0, wide_count, rows_dev)
    keep_b, send_b = project(
        values, out_proj, order, cols, None, tile, wide_count, narrow_count, rows_dev
    )
    mid_a, row_a = payload(reduce_plane_first(net, keep_a, send_a, rows_dev), 0, wide)
    mid_b, row_b = payload(reduce_line_first(net, keep_b, send_b, rows_dev), wide, slice_width)
    pieces_a = gather_line_first(net, row_a)
    pieces_b = gather_plane_first(net, row_b)

    mine = me.reshape(1).astype(jnp.int32)
    before = gate_up(
        net, pieces_b, True, gate_w[0], up_w[0], cols, mine, tile, wide_count, narrow_count, rows_dev
    )
    hidden, coef = gate_up(
        net, pieces_a, False, gate_w[0], up_w[0], cols, mine, tile, 0, wide_count, rows_dev, before
    )
    keep_a, send_a = project(hidden, down_w[0], natural, cols, coef, tile, 0, wide_count, rows_dev)
    keep_b, send_b = project(
        hidden, down_w[0], natural, cols, coef, tile, wide_count, narrow_count, rows_dev
    )
    out_a = mid_a + reduce_plane_first(net, keep_a, send_a, rows_dev)
    out_b = mid_b + reduce_line_first(net, keep_b, send_b, rows_dev)
    return jnp.concatenate([out_a, out_b], 1).astype(BF16)


def solution(mesh):
    return jax.shard_map(
        on_device,
        mesh=mesh,
        in_specs=(
            P(("groups", "dp"), "heads", None),
            P(("groups", "dp"), None, None),
            P(("groups", "dp")),
            P(("groups", "dp"), None),
            P("heads", "dp", None, None),
            P("heads", "dp", None, None),
            P(),
            P(("groups", "dp"), None),
            P(("groups", "dp"), None),
            P(),
            P("dp", None, "heads"),
            P("dp", None, "heads"),
            P("dp", "heads", None),
        ),
        out_specs=P(("groups", "dp"), "heads"),
        check_vma=False,
    )
```

```python
import functools

import jax
import jax.numpy as jnp
from jax import lax
from jax.experimental import pallas as pl
from jax.experimental.pallas import tpu as pltpu
from jax.sharding import PartitionSpec as P

LAT = 512
EPSILON = 1e-06
SCORE_SCALE = 192.0 ** (-0.5)
BF16 = jnp.bfloat16
F32 = jnp.float32
EXTRA = 128
PROJECT_BYTES = 12 * 1024 * 1024
EXPERT_BYTES = 16 * 1024 * 1024
PAYLOAD_BYTES = 4 * 1024 * 1024


def attend_kernel(lengths, q_ref, cache_ref, out_ref, *, rows, latent):
    positions = lax.broadcasted_iota(jnp.int32, (1, cache_ref.shape[2]), 1)
    scores = [
        jnp.dot(q_ref[row], cache_ref[row], preferred_element_type=F32) * SCORE_SCALE
        for row in range(rows)
    ]
    weights = []
    for row in range(rows):
        live = positions < lengths[pl.program_id(0) * rows + row]
        score = jnp.where(live, scores[row], -jnp.inf)
        weight = jnp.exp(score - jnp.max(score, -1, keepdims=True))
        weights.append((weight / jnp.sum(weight, -1, keepdims=True)).astype(BF16))
    for row in range(rows):
        mixed = lax.dot_general(
            weights[row],
            cache_ref[row, :latent],
            (((1,), (1,)), ((), ())),
            preferred_element_type=F32,
        )
        out_ref[row] = mixed.astype(BF16)


def attend(queries, kv_cache, lengths):
    count, heads, depth = queries.shape
    context = kv_cache.shape[1]
    cache = jnp.swapaxes(kv_cache, 1, 2)
    rows = 4
    return pl.pallas_call(
        functools.partial(attend_kernel, rows=rows, latent=LAT),
        grid=(count // rows,),
        in_specs=[
            pl.BlockSpec(memory_space=pltpu.SMEM),
            pl.BlockSpec((rows, heads, depth), lambda i: (i, 0, 0)),
            pl.BlockSpec((rows, depth, context), lambda i: (i, 0, 0)),
        ],
        out_specs=pl.BlockSpec((rows, heads, LAT), lambda i: (i, 0, 0)),
        out_shape=jax.ShapeDtypeStruct((count, heads, LAT), BF16),
        compiler_params=pltpu.CompilerParams(vmem_limit_bytes=57 * 1024 * 1024),
    )(lengths, queries, cache)


class Net:
    def __init__(self, dp, heads):
        self.dp, self.heads = dp, heads
        self.near = 2
        self.line = dp // 4
        self.plane = [(jh, jx) for jh in range(heads) for jx in range(self.near)]

    def move(self, value, dp_mask, heads_mask=0):
        mask = dp_mask * self.heads + heads_mask
        count = self.dp * self.heads
        return lax.ppermute(value, ("dp", "heads"), [(i, i ^ mask) for i in range(count)])

    def core(self, value):
        return self.move(value, 1)

    def in_plane(self, value, at):
        jh, jx = self.plane[at]
        return self.move(value, 2 * jx, jh)

    def in_line(self, value, jz):
        return self.move(value, 4 * jz)


def values_kernel(order, latent_ref, map_ref, out_ref, x_scr):
    sources, heads, rows, _ = latent_ref.shape
    wide = map_ref.shape[-1]
    for head in range(heads):
        for slot in range(sources):
            x_scr[slot * rows : (slot + 1) * rows, :] = latent_ref[order[slot], head]
        out = jnp.dot(x_scr[...], map_ref[head], preferred_element_type=F32)
        out_ref[:, head * wide : (head + 1) * wide] = out.astype(BF16)


def values_of(latents, maps, order):
    sources, heads, rows, latent = latents.shape
    vmem = pl.BlockSpec(memory_space=pltpu.VMEM)
    return pl.pallas_call(
        values_kernel,
        in_specs=[pl.BlockSpec(memory_space=pltpu.SMEM), vmem, vmem],
        out_specs=vmem,
        out_shape=jax.ShapeDtypeStruct((sources * rows, heads * maps.shape[-1]), BF16),
        scratch_shapes=[pltpu.VMEM((sources * rows, latent), BF16)],
        compiler_params=pltpu.CompilerParams(vmem_limit_bytes=16 * 1024 * 1024),
    )(order, latents, maps)


def put(out, keep_ref, send_ref, head, lanes):
    half = out.shape[0] // 2
    keep_ref[head, :, lanes] = out[:half].astype(BF16)
    send_ref[head, :, lanes] = out[half:].astype(BF16)


def column_lanes(cols, h, tile, first, t, slice_width):
    return pl.ds(pl.multiple_of(cols[h] * slice_width + (first + t) * tile, 128), tile)


def project_kernel(cols, *refs, tile, first, count, scaled):
    if scaled:
        x_ref, scale_ref, *refs = refs
    else:
        x_ref, *refs = refs
    w_ref, keep_ref, send_ref = refs
    heads = keep_ref.shape[0]
    slice_width = w_ref.shape[1] // heads
    for h in range(heads):
        for t in range(count):
            lanes = column_lanes(cols, h, tile, first, t, slice_width)
            out = jnp.dot(x_ref[...], w_ref[:, lanes], preferred_element_type=F32)
            if scaled:
                out = out * scale_ref[:, :1]
            put(out, keep_ref, send_ref, h, slice(t * tile, (t + 1) * tile))


def project(x, weights, cols, scale, tile, first, count):
    rows, depth = x.shape
    heads = cols.shape[0]
    out = jax.ShapeDtypeStruct((heads, rows // 2, count * tile), BF16)
    given = [x] if scale is None else [x, scale]
    vmem = pl.BlockSpec(memory_space=pltpu.VMEM)
    smem = pl.BlockSpec(memory_space=pltpu.SMEM)
    return pl.pallas_call(
        functools.partial(
            project_kernel, tile=tile, first=first, count=count, scaled=scale is not None
        ),
        in_specs=[smem] + [vmem] * (len(given) + 1),
        out_specs=[vmem, vmem],
        out_shape=[out, out],
        compiler_params=pltpu.CompilerParams(vmem_limit_bytes=PROJECT_BYTES),
        cost_estimate=pl.CostEstimate(
            flops=2 * rows * depth * count * tile * heads,
            bytes_accessed=2 * (depth + rows) * count * tile * heads,
            transcendentals=0,
        ),
    )(cols, *given, weights)


def pieces_of(value):
    high = lax.reduce_precision(value, 8, 7)
    rest = value - high
    middle = lax.reduce_precision(rest, 8, 7)
    return [high.astype(BF16), middle.astype(BF16), (rest - middle).astype(BF16)]


def row_parts(pieces, jh, net, by_line, rows_dev, lanes):
    parts = []
    for jc in range(2):
        for jx in range(net.near):
            at = jh * net.near + jx
            if by_line:
                for jz in range(net.line):
                    ref = pieces[jc][jz]
                    parts.append(ref[at * rows_dev : (at + 1) * rows_dev, lanes])
            else:
                parts.append(pieces[jc][at][:, lanes])
    return jnp.concatenate(parts, 0)


def expert_kernel(cols, me, *refs, net, groups, rows_dev, tile, counts, width):
    pieces = []
    for per_core in groups:
        pieces.append([refs[:per_core], refs[per_core : 2 * per_core]])
        refs = refs[2 * per_core :]
    gate_ref, up_ref, down_ref, hidden_ref, coef_ref, keep_ref, send_ref, gate_acc, up_acc = refs
    heads = net.heads
    slice_width = width // heads
    plan = [
        (group, jh, t, (0 if group == 0 else counts[0]) + t)
        for group in (1, 0)
        for jh in range(heads)
        for t in range(counts[group])
    ]
    for at, (group, jh, t, in_slice) in enumerate(plan):
        x = row_parts(pieces[group], jh, net, group == 1, rows_dev, slice(t * tile, (t + 1) * tile))
        row = pl.ds(pl.multiple_of(cols[jh] * slice_width + in_slice * tile, 128), tile)
        gate = jnp.dot(x, gate_ref[row, :], preferred_element_type=F32)
        up = jnp.dot(x, up_ref[row, :], preferred_element_type=F32)
        if at == 0:
            gate_acc[...] = gate
            up_acc[...] = up
        else:
            gate_acc[...] += gate
            up_acc[...] += up

    lane = lax.broadcasted_iota(jnp.int32, (1, EXTRA), 1)
    squares = 0.0
    for group in range(2):
        lanes = slice(counts[group] * tile, counts[group] * tile + EXTRA)
        for jh in range(heads):
            extra = row_parts(pieces[group], jh, net, group == 1, rows_dev, lanes).astype(F32)
            squares = squares + extra
    squares = jnp.sum(jnp.where(lane < 3, squares, 0.0), -1, keepdims=True)
    norm = lax.rsqrt(squares / width + EPSILON)
    mine = (lane == 3 + me[0]) | (lane == 3 + net.dp + me[0]) | (lane == 3 + 2 * net.dp + me[0])
    coef = jnp.sum(jnp.where(mine, extra, 0.0), -1, keepdims=True)
    coef_ref[...] = jnp.broadcast_to(coef, coef_ref.shape)
    gate = gate_acc[...] * norm
    up = up_acc[...] * norm
    hidden_ref[...] = (gate / (1.0 + jnp.exp(-gate)) * up).astype(BF16)
    for h in range(heads):
        for t in range(counts[0]):
            lanes = column_lanes(cols, h, tile, 0, t, slice_width)
            out = jnp.dot(hidden_ref[...], down_ref[:, lanes], preferred_element_type=F32) * coef
            put(out, keep_ref, send_ref, h, slice(t * tile, (t + 1) * tile))


def experts_of(net, pieces_a, pieces_b, gate_w, up_w, down_w, cols, me, tile, counts, rows_dev):
    flat = [piece for pieces in (pieces_a, pieces_b) for group in pieces for piece in group]
    width, hidden = gate_w.shape
    rows = net.dp * rows_dev
    heads = net.heads
    vmem = pl.BlockSpec(memory_space=pltpu.VMEM)
    smem = pl.BlockSpec(memory_space=pltpu.SMEM)
    out = jax.ShapeDtypeStruct((heads, rows // 2, counts[0] * tile), BF16)
    return pl.pallas_call(
        functools.partial(
            expert_kernel,
            net=net,
            groups=(len(pieces_a[0]), len(pieces_b[0])),
            rows_dev=rows_dev,
            tile=tile,
            counts=counts,
            width=width,
        ),
        in_specs=[smem, smem] + [vmem] * (len(flat) + 3),
        out_specs=[vmem] * 4,
        out_shape=[
            jax.ShapeDtypeStruct((rows, hidden), BF16),
            jax.ShapeDtypeStruct((rows, EXTRA), F32),
            out,
            out,
        ],
        scratch_shapes=[
            pltpu.VMEM((rows, hidden), F32),
            pltpu.VMEM((rows, hidden), F32),
        ],
        compiler_params=pltpu.CompilerParams(vmem_limit_bytes=EXPERT_BYTES),
        cost_estimate=pl.CostEstimate(
            flops=6 * rows * width * hidden,
            bytes_accessed=6 * width * hidden,
            transcendentals=0,
        ),
    )(cols, me, *flat, gate_w, up_w, down_w)


def payload_kernel(*refs, arrived, width):
    own, rest = refs[:2], refs[2:]
    received, rest = [rest[: arrived[0]], rest[arrived[0] : sum(arrived)]], rest[sum(arrived) :]
    resid_ref, gain_ref, extra_ref = rest[:3]
    mids, rows = rest[3:5], rest[5:7]
    lane = lax.broadcasted_iota(jnp.int32, (1, EXTRA), 1)
    start = 0
    for which in range(2):
        total = own[which][...]
        for ref in received[which]:
            total = total + ref[...].astype(F32)
        size = total.shape[-1]
        mid = resid_ref[:, start : start + size].astype(F32) + total
        mids[which][...] = mid
        rows[which][:, :size] = (mid * gain_ref[:, start : start + size].astype(F32)).astype(BF16)
        squares = jnp.sum(mid * mid, -1, keepdims=True)
        high = squares.astype(BF16)
        left = squares - high.astype(F32)
        middle = left.astype(BF16)
        low = (left - middle.astype(F32)).astype(BF16)
        extra = extra_ref[...]
        for at, part in enumerate((high, middle, low)):
            extra = jnp.where(lane == at, jnp.broadcast_to(part, extra.shape), extra)
        rows[which][:, size:] = extra
        start += size


def payloads(parts_a, parts_b, resid, gain, extra):
    own_a, in_a = parts_a
    own_b, in_b = parts_b
    rows = own_a.shape[0]
    mids = [jax.ShapeDtypeStruct(own.shape, F32) for own in (own_a, own_b)]
    outs = [jax.ShapeDtypeStruct((rows, own.shape[1] + EXTRA), BF16) for own in (own_a, own_b)]
    operands = [own_a, own_b, *in_a, *in_b, resid, gain, extra]
    vmem = pl.BlockSpec(memory_space=pltpu.VMEM)
    return pl.pallas_call(
        functools.partial(
            payload_kernel, arrived=(len(in_a), len(in_b)), width=resid.shape[1]
        ),
        in_specs=[vmem] * len(operands),
        out_specs=[vmem] * 4,
        out_shape=mids + outs,
        compiler_params=pltpu.CompilerParams(vmem_limit_bytes=PAYLOAD_BYTES),
    )(*operands)


def summed_with(own, arrived):
    for value in arrived:
        own = own + value.astype(F32)
    return own


def reduce_both(net, first, second, rows_dev):
    places, line = len(net.plane), net.line
    (keep_a, send_a), (keep_b, send_b) = first, second
    other_a, other_b = net.core(send_a), net.core(send_b)
    shape_a = (places, line * rows_dev, keep_a.shape[-1])
    shape_b = (places, line, rows_dev, keep_b.shape[-1])
    keep_a, other_a = keep_a.reshape(shape_a), other_a.reshape(shape_a)
    keep_b, other_b = keep_b.reshape(shape_b), other_b.reshape(shape_b)
    sum_a = [keep_a[at].astype(F32) + other_a[at].astype(F32) for at in range(places)]
    sum_b = [keep_b[:, jz].astype(F32) + other_b[:, jz].astype(F32) for jz in range(line)]
    go_a = [value.astype(BF16) for value in sum_a[1:]]
    go_b = [value.astype(BF16) for value in sum_b[1:]]
    go_a, go_b = lax.optimization_barrier((go_a, go_b))
    in_b = [net.in_line(value, jz + 1) for jz, value in enumerate(go_b)]
    in_a = [net.in_plane(value, at + 1) for at, value in enumerate(go_a)]
    sum_a = summed_with(sum_a[0], in_a).reshape(line, rows_dev, keep_a.shape[-1])
    sum_b = summed_with(sum_b[0], in_b)
    go_a = [sum_a[jz].astype(BF16) for jz in range(1, line)]
    go_b = [sum_b[at].astype(BF16) for at in range(1, places)]
    go_a, go_b = lax.optimization_barrier((go_a, go_b))
    in_b = [net.in_plane(value, at + 1) for at, value in enumerate(go_b)]
    in_a = [net.in_line(value, jz + 1) for jz, value in enumerate(go_a)]
    return (sum_a[0], in_a), (sum_b[0], in_b)


def gather_both(net, row_a, row_b):
    places, line = len(net.plane), net.line
    row_a, row_b = lax.optimization_barrier((row_a, row_b))
    in_b = [net.in_plane(row_b, at) for at in range(1, places)]
    in_a = [net.in_line(row_a, jz) for jz in range(1, line)]
    held_a = jnp.concatenate([row_a] + in_a, 0)
    held_b = jnp.concatenate([row_b] + in_b, 0)
    held_a, held_b = lax.optimization_barrier((held_a, held_b))
    own_b = [held_b] + [net.in_line(held_b, jz) for jz in range(1, line)]
    own_a = [held_a] + [net.in_plane(held_a, at) for at in range(1, places)]
    return [own_a, [net.core(piece) for piece in own_a]], [own_b, [net.core(piece) for piece in own_b]]


def on_device(
    queries,
    kv_cache,
    lengths,
    resid,
    w_uv,
    o_proj,
    norm_gain,
    expert_ids,
    route_gates,
    expert_owner,
    gate_w,
    up_w,
    down_w,
):
    dp = lax.axis_size("dp")
    heads = lax.axis_size("heads")
    net = Net(dp, heads)
    rows_dev, width = resid.shape
    slice_width = width // heads
    tile = slice_width // 7
    wide_count, narrow_count = 5, 2
    me = lax.axis_index("dp")
    my_head = lax.axis_index("heads")
    slots = jnp.array(
        [
            jc + 2 * jx + 4 * jz
            for jc in range(2)
            for jx in range(net.near)
            for jz in range(net.line)
        ],
        jnp.int32,
    )
    order = jnp.bitwise_xor(slots, me)
    natural = jnp.arange(dp, dtype=jnp.int32)
    cols = jnp.bitwise_xor(jnp.arange(heads, dtype=jnp.int32), my_head)

    latent_out = attend(queries, kv_cache, lengths)
    gathered = lax.all_to_all(
        jnp.swapaxes(latent_out, 0, 1), "dp", split_axis=0, concat_axis=0, tiled=True
    )
    gathered = gathered.reshape(dp, -1, rows_dev, LAT)
    out_proj = o_proj[0].reshape(-1, width)

    holder = jnp.sum(
        (expert_ids[:, :, None] == jnp.arange(expert_owner.shape[0], dtype=jnp.int32)).astype(jnp.int32)
        * expert_owner,
        -1,
    )
    table = jnp.sum(jnp.where(holder[:, :, None] == natural, route_gates[:, :, None], 0.0), 1)
    table_parts = pieces_of(table)

    resid_slice = lax.dynamic_slice_in_dim(resid, my_head * slice_width, slice_width, 1)
    gain_slice = lax.dynamic_slice_in_dim(norm_gain, my_head * slice_width, slice_width, 0)
    extra = jnp.concatenate([jnp.zeros((rows_dev, 3), BF16), *table_parts], 1)
    extra = jnp.pad(extra, ((0, 0), (0, EXTRA - extra.shape[1])))

    gain_slice = gain_slice.reshape(1, -1)
    mine = me.reshape(1).astype(jnp.int32)
    gathered, resid_slice, gain_slice, extra, order, cols, mine = lax.optimization_barrier(
        (gathered, resid_slice, gain_slice, extra, order, cols, mine)
    )
    values = values_of(gathered, w_uv[0], order)
    keep_a, send_a = project(values, out_proj, cols, None, tile, 0, wide_count)
    keep_b, send_b = project(values, out_proj, cols, None, tile, wide_count, narrow_count)
    parts_a, parts_b = reduce_both(net, (keep_a, send_a), (keep_b, send_b), rows_dev)
    mid_a, mid_b, row_a, row_b = payloads(
        parts_a, parts_b, resid_slice, gain_slice, extra
    )
    pieces_a, pieces_b = gather_both(net, row_a, row_b)

    hidden, coef, keep_a, send_a = experts_of(
        net,
        pieces_a,
        pieces_b,
        gate_w[0],
        up_w[0],
        down_w[0],
        cols,
        mine,
        tile,
        (wide_count, narrow_count),
        rows_dev,
    )
    keep_b, send_b = project(hidden, down_w[0], cols, coef, tile, wide_count, narrow_count)
    moe_a, moe_b = reduce_both(net, (keep_a, send_a), (keep_b, send_b), rows_dev)
    return jnp.concatenate(
        [mid_a + summed_with(*moe_a), mid_b + summed_with(*moe_b)], 1
    ).astype(BF16)


def solution(mesh):
    return jax.shard_map(
        on_device,
        mesh=mesh,
        in_specs=(
            P(("groups", "dp"), "heads", None),
            P(("groups", "dp"), None, None),
            P(("groups", "dp")),
            P(("groups", "dp"), None),
            P("heads", "dp", None, None),
            P("heads", "dp", None, None),
            P(),
            P(("groups", "dp"), None),
            P(("groups", "dp"), None),
            P(),
            P("dp", None, "heads"),
            P("dp", None, "heads"),
            P("dp", "heads", None),
        ),
        out_specs=P(("groups", "dp"), "heads"),
        check_vma=False,
    )
```

```python
import functools

import jax
import jax.numpy as jnp
from jax import lax
from jax.experimental import pallas as pl
from jax.experimental.pallas import tpu as pltpu
from jax.sharding import PartitionSpec as P

LAT = 512
EPSILON = 1e-06
SCORE_SCALE = 192.0 ** (-0.5)
BF16 = jnp.bfloat16
F32 = jnp.float32
EXTRA = 128
PROJECT_BYTES = 12 * 1024 * 1024
EXPERT_BYTES = 16 * 1024 * 1024
PAYLOAD_BYTES = 4 * 1024 * 1024


def attend_kernel(lengths, q_ref, cache_ref, out_ref, *scrs, rows, latent):
    heads = q_ref.shape[1]
    positions = lax.broadcasted_iota(jnp.int32, (1, cache_ref.shape[2]), 1)
    scores = [
        jnp.dot(q_ref[row], cache_ref[row], preferred_element_type=F32) * SCORE_SCALE
        for row in range(rows)
    ]
    weights = []
    for row in range(rows):
        live = positions < lengths[pl.program_id(0) * rows + row]
        score = jnp.where(live, scores[row], -jnp.inf)
        weight = jnp.exp(score - jnp.max(score, -1, keepdims=True))
        weights.append((weight / jnp.sum(weight, -1, keepdims=True)).astype(BF16))
    for row in range(rows):
        mixed = lax.dot_general(
            weights[row],
            cache_ref[row, :latent],
            (((1,), (1,)), ((), ())),
            preferred_element_type=F32,
        )
        at = (pl.program_id(0) * rows + row) * heads
        for part, scr in enumerate(scrs):
            scr[pl.ds(pl.multiple_of(at, 8), heads), :] = mixed[:, part * 128 : (part + 1) * 128]

    @pl.when(pl.program_id(0) == pl.num_programs(0) - 1)
    def _():
        for head in range(heads):
            for part, scr in enumerate(scrs):
                out_ref[head, :, part * 128 : (part + 1) * 128] = scr[
                    pl.ds(head, out_ref.shape[1], stride=heads), :
                ].astype(BF16)


def attend(queries, kv_cache, lengths):
    count, heads, depth = queries.shape
    context = kv_cache.shape[1]
    cache = jnp.swapaxes(kv_cache, 1, 2)
    rows = 4
    return pl.pallas_call(
        functools.partial(attend_kernel, rows=rows, latent=LAT),
        grid=(count // rows,),
        in_specs=[
            pl.BlockSpec(memory_space=pltpu.SMEM),
            pl.BlockSpec((rows, heads, depth), lambda i: (i, 0, 0)),
            pl.BlockSpec((rows, depth, context), lambda i: (i, 0, 0)),
        ],
        out_specs=pl.BlockSpec(memory_space=pltpu.VMEM),
        out_shape=jax.ShapeDtypeStruct((heads, count, LAT), BF16),
        scratch_shapes=[pltpu.VMEM((count * heads, 128), F32)] * (LAT // 128),
        compiler_params=pltpu.CompilerParams(vmem_limit_bytes=56 * 1024 * 1024),
    )(lengths, queries, cache)


class Net:
    def __init__(self, dp, heads):
        self.dp, self.heads = dp, heads
        self.near = 2
        self.line = dp // 4
        self.plane = [(jh, jx) for jh in range(heads) for jx in range(self.near)]
        self.line_bits = self.line.bit_length() - 1
        self.plane_bits = len(self.plane).bit_length() - 1
        slots = [0]
        for bit in reversed(range(1, self.line_bits)):
            slots = slots + [slot | 1 << bit for slot in slots]
        self.line_at = {slot | odd: (odd, at) for odd in range(2) for at, slot in enumerate(slots)}

    def move(self, value, dp_mask, heads_mask=0):
        mask = dp_mask * self.heads + heads_mask
        count = self.dp * self.heads
        return lax.ppermute(value, ("dp", "heads"), [(i, i ^ mask) for i in range(count)])

    def core(self, value):
        return self.move(value, 1)

    def in_plane(self, value, at):
        jh, jx = self.plane[at]
        return self.move(value, 2 * jx, jh)

    def in_line(self, value, jz):
        return self.move(value, 4 * jz)


def values_kernel(order, latent_ref, map_ref, out_ref, x_scr):
    sources, heads, rows, _ = latent_ref.shape
    wide = map_ref.shape[-1]
    for head in range(heads):
        for slot in range(sources):
            x_scr[slot * rows : (slot + 1) * rows, :] = latent_ref[order[slot], head]
        out = jnp.dot(x_scr[...], map_ref[head], preferred_element_type=F32)
        out_ref[:, head * wide : (head + 1) * wide] = out.astype(BF16)


def values_of(latents, maps, order):
    sources, heads, rows, latent = latents.shape
    vmem = pl.BlockSpec(memory_space=pltpu.VMEM)
    return pl.pallas_call(
        values_kernel,
        in_specs=[pl.BlockSpec(memory_space=pltpu.SMEM), vmem, vmem],
        out_specs=vmem,
        out_shape=jax.ShapeDtypeStruct((sources * rows, heads * maps.shape[-1]), BF16),
        scratch_shapes=[pltpu.VMEM((sources * rows, latent), BF16)],
        compiler_params=pltpu.CompilerParams(vmem_limit_bytes=16 * 1024 * 1024),
    )(order, latents, maps)


def put(out, keep_ref, send_ref, head, lanes):
    half = out.shape[0] // 2
    keep_ref[head, :, lanes] = out[:half].astype(BF16)
    send_ref[head, :, lanes] = out[half:].astype(BF16)


def column_lanes(cols, h, tile, first, t, slice_width):
    return pl.ds(pl.multiple_of(cols[h] * slice_width + (first + t) * tile, 128), tile)


def project_kernel(cols, *refs, tile, first, count, scaled):
    if scaled:
        x_ref, scale_ref, *refs = refs
    else:
        x_ref, *refs = refs
    w_ref, keep_ref, send_ref = refs
    heads = keep_ref.shape[0]
    slice_width = w_ref.shape[1] // heads
    for h in range(heads):
        for t in range(count):
            lanes = column_lanes(cols, h, tile, first, t, slice_width)
            out = jnp.dot(x_ref[...], w_ref[:, lanes], preferred_element_type=F32)
            if scaled:
                out = out * scale_ref[:, :1]
            put(out, keep_ref, send_ref, h, slice(t * tile, (t + 1) * tile))


def project(x, weights, cols, scale, tile, first, count):
    rows, depth = x.shape
    heads = cols.shape[0]
    out = jax.ShapeDtypeStruct((heads, rows // 2, count * tile), BF16)
    given = [x] if scale is None else [x, scale]
    vmem = pl.BlockSpec(memory_space=pltpu.VMEM)
    smem = pl.BlockSpec(memory_space=pltpu.SMEM)
    return pl.pallas_call(
        functools.partial(
            project_kernel, tile=tile, first=first, count=count, scaled=scale is not None
        ),
        in_specs=[smem] + [vmem] * (len(given) + 1),
        out_specs=[vmem, vmem],
        out_shape=[out, out],
        compiler_params=pltpu.CompilerParams(vmem_limit_bytes=PROJECT_BYTES),
        cost_estimate=pl.CostEstimate(
            flops=2 * rows * depth * count * tile * heads,
            bytes_accessed=2 * (depth + rows) * count * tile * heads,
            transcendentals=0,
        ),
    )(cols, *given, weights)


def pieces_of(value):
    high = lax.reduce_precision(value, 8, 7)
    rest = value - high
    middle = lax.reduce_precision(rest, 8, 7)
    return [high.astype(BF16), middle.astype(BF16), (rest - middle).astype(BF16)]


def row_parts(pieces, jh, net, by_line, rows_dev, lanes):
    parts = []
    for jc in range(2):
        for jx in range(net.near):
            at = jh * net.near + jx
            if by_line:
                for jz in range(net.line):
                    piece, index = net.line_at[jz]
                    start = (index * len(net.plane) + at) * rows_dev
                    parts.append(pieces[jc][piece][start : start + rows_dev, lanes])
            else:
                parts.append(pieces[jc][at][:, lanes])
    return jnp.concatenate(parts, 0)


def expert_kernel(cols, me, *refs, net, groups, rows_dev, tile, counts, width):
    pieces = []
    for per_core in groups:
        pieces.append([refs[:per_core], refs[per_core : 2 * per_core]])
        refs = refs[2 * per_core :]
    gate_ref, up_ref, down_ref, hidden_ref, coef_ref, keep_ref, send_ref, gate_acc, up_acc = refs
    heads = net.heads
    slice_width = width // heads
    plan = [
        (group, jh, t, (0 if group == 0 else counts[0]) + t)
        for group in (1, 0)
        for jh in range(heads)
        for t in range(counts[group])
    ]
    for at, (group, jh, t, in_slice) in enumerate(plan):
        x = row_parts(pieces[group], jh, net, group == 1, rows_dev, slice(t * tile, (t + 1) * tile))
        row = pl.ds(pl.multiple_of(cols[jh] * slice_width + in_slice * tile, 128), tile)
        gate = jnp.dot(x, gate_ref[row, :], preferred_element_type=F32)
        up = jnp.dot(x, up_ref[row, :], preferred_element_type=F32)
        if at == 0:
            gate_acc[...] = gate
            up_acc[...] = up
        else:
            gate_acc[...] += gate
            up_acc[...] += up

    lane = lax.broadcasted_iota(jnp.int32, (1, EXTRA), 1)
    squares = 0.0
    lanes = slice(counts[1] * tile, counts[1] * tile + EXTRA)
    for jh in range(heads):
        extra = row_parts(pieces[1], jh, net, True, rows_dev, lanes).astype(F32)
        squares = squares + extra
    squares = jnp.sum(jnp.where(lane < 3, squares, 0.0), -1, keepdims=True)
    norm = lax.rsqrt(squares / width + EPSILON)
    mine = (lane == 3 + me[0]) | (lane == 3 + net.dp + me[0]) | (lane == 3 + 2 * net.dp + me[0])
    coef = jnp.sum(jnp.where(mine, extra, 0.0), -1, keepdims=True)
    coef_ref[...] = jnp.broadcast_to(coef, coef_ref.shape)
    gate = gate_acc[...] * norm
    up = up_acc[...] * norm
    hidden_ref[...] = (gate / (1.0 + jnp.exp(-gate)) * up).astype(BF16)
    for h in range(heads):
        for t in range(counts[0]):
            lanes = column_lanes(cols, h, tile, 0, t, slice_width)
            out = jnp.dot(hidden_ref[...], down_ref[:, lanes], preferred_element_type=F32) * coef
            put(out, keep_ref, send_ref, h, slice(t * tile, (t + 1) * tile))


def experts_of(net, pieces_a, pieces_b, gate_w, up_w, down_w, cols, me, tile, counts, rows_dev):
    flat = [piece for pieces in (pieces_a, pieces_b) for group in pieces for piece in group]
    width, hidden = gate_w.shape
    rows = net.dp * rows_dev
    heads = net.heads
    vmem = pl.BlockSpec(memory_space=pltpu.VMEM)
    smem = pl.BlockSpec(memory_space=pltpu.SMEM)
    out = jax.ShapeDtypeStruct((heads, rows // 2, counts[0] * tile), BF16)
    return pl.pallas_call(
        functools.partial(
            expert_kernel,
            net=net,
            groups=(len(pieces_a[0]), len(pieces_b[0])),
            rows_dev=rows_dev,
            tile=tile,
            counts=counts,
            width=width,
        ),
        in_specs=[smem, smem] + [vmem] * (len(flat) + 3),
        out_specs=[vmem] * 4,
        out_shape=[
            jax.ShapeDtypeStruct((rows, hidden), BF16),
            jax.ShapeDtypeStruct((rows, EXTRA), F32),
            out,
            out,
        ],
        scratch_shapes=[
            pltpu.VMEM((rows, hidden), F32),
            pltpu.VMEM((rows, hidden), F32),
        ],
        compiler_params=pltpu.CompilerParams(vmem_limit_bytes=EXPERT_BYTES),
        cost_estimate=pl.CostEstimate(
            flops=6 * rows * width * hidden,
            bytes_accessed=6 * width * hidden,
            transcendentals=0,
        ),
    )(cols, me, *flat, gate_w, up_w, down_w)


def payload_kernel(*refs, arrived, width):
    own, rest = refs[:2], refs[2:]
    received, rest = [rest[: arrived[0]], rest[arrived[0] : sum(arrived)]], rest[sum(arrived) :]
    resid_ref, gain_ref, extra_ref = rest[:3]
    mids, rows = rest[3:5], rest[5:7]
    lane = lax.broadcasted_iota(jnp.int32, (1, EXTRA), 1)
    start = 0
    squares = 0.0
    for which in range(2):
        total = own[which][...]
        for ref in received[which]:
            total = total + ref[...].astype(F32)
        size = total.shape[-1]
        mid = resid_ref[:, start : start + size].astype(F32) + total
        mids[which][...] = mid
        rows[which][:, :size] = (mid * gain_ref[:, start : start + size].astype(F32)).astype(BF16)
        squares = squares + jnp.sum(mid * mid, -1, keepdims=True)
        start += size
    high = squares.astype(BF16)
    left = squares - high.astype(F32)
    middle = left.astype(BF16)
    low = (left - middle.astype(F32)).astype(BF16)
    extra = extra_ref[...]
    for at, part in enumerate((high, middle, low)):
        extra = jnp.where(lane == at, jnp.broadcast_to(part, extra.shape), extra)
    rows[1][:, size:] = extra


def payloads(parts_a, parts_b, resid, gain, extra):
    own_a, in_a = parts_a
    own_b, in_b = parts_b
    rows = own_a.shape[0]
    mids = [jax.ShapeDtypeStruct(own.shape, F32) for own in (own_a, own_b)]
    outs = [
        jax.ShapeDtypeStruct((rows, own_a.shape[1]), BF16),
        jax.ShapeDtypeStruct((rows, own_b.shape[1] + EXTRA), BF16),
    ]
    operands = [own_a, own_b, *in_a, *in_b, resid, gain, extra]
    vmem = pl.BlockSpec(memory_space=pltpu.VMEM)
    return pl.pallas_call(
        functools.partial(
            payload_kernel, arrived=(len(in_a), len(in_b)), width=resid.shape[1]
        ),
        in_specs=[vmem] * len(operands),
        out_specs=[vmem] * 4,
        out_shape=mids + outs,
        compiler_params=pltpu.CompilerParams(vmem_limit_bytes=PAYLOAD_BYTES),
    )(*operands)


def summed_with(own, arrived):
    for value in arrived:
        own = own + value.astype(F32)
    return own


def reduce_both(net, first, second, rows_dev):
    places, line = len(net.plane), net.line
    (keep_a, send_a), (keep_b, send_b) = first, second
    other_a, other_b = net.core(send_a), net.core(send_b)
    shape_a = (places, line * rows_dev, keep_a.shape[-1])
    shape_b = (places, line, rows_dev, keep_b.shape[-1])
    keep_a, other_a = keep_a.reshape(shape_a), other_a.reshape(shape_a)
    keep_b, other_b = keep_b.reshape(shape_b), other_b.reshape(shape_b)
    sum_a = [keep_a[at].astype(F32) + other_a[at].astype(F32) for at in range(places)]
    sum_b = {jz: keep_b[:, jz].astype(F32) + other_b[:, jz].astype(F32) for jz in range(line)}
    go_a = [value.astype(BF16) for value in sum_a[1:]]
    go_b = [sum_b[jz].astype(BF16) for jz in range(1, line)]
    go_a, go_b = lax.optimization_barrier((go_a, go_b))
    in_b = [net.in_line(value, jz + 1) for jz, value in enumerate(go_b)]
    in_a = [net.in_plane(value, at + 1) for at, value in enumerate(go_a)]
    sum_a = summed_with(sum_a[0], in_a).reshape(line, rows_dev, keep_a.shape[-1])
    sum_a, in_b = lax.optimization_barrier((sum_a, in_b))
    sum_b = summed_with(sum_b[0], in_b)
    go_a = [sum_a[jz].astype(BF16) for jz in range(1, line)]
    sum_b = {at: sum_b[at] for at in range(places)}
    go_b, sum_b = split_pairs(sum_b, 0)
    go_a, go_b = lax.optimization_barrier((go_a, go_b))
    for bit in range(net.plane_bits):
        if bit:
            go_b, sum_b = split_pairs(sum_b, bit)
        last = net.in_plane(go_b, 1 << bit)
        if bit < net.plane_bits - 1:
            sum_b = join_pairs(sum_b, last)
    in_a = [net.in_line(value, jz + 1) for jz, value in enumerate(go_a)]
    return (sum_a[0], in_a), (sum_b[0], [last.reshape(rows_dev, -1)])


def split_pairs(parts, bit):
    go = jnp.stack([parts[slot].astype(BF16) for slot in sorted(parts) if slot >> bit & 1])
    return go, {slot: value for slot, value in parts.items() if not slot >> bit & 1}


def join_pairs(parts, arrived):
    return {slot: parts[slot] + arrived[at].astype(F32) for at, slot in enumerate(sorted(parts))}


def gather_both(net, row_a, row_b):
    places, line = len(net.plane), net.line
    row_a, row_b = lax.optimization_barrier((row_a, row_b))
    held_b = row_b
    for bit in range(net.plane_bits):
        held_b = jnp.concatenate([held_b, net.in_plane(held_b, 1 << bit)], 0)
    in_a = [net.in_line(row_a, jz) for jz in range(1, line)]
    held_a = jnp.concatenate([row_a] + in_a, 0)
    held_a, held_b = lax.optimization_barrier((held_a, held_b))
    for bit in reversed(range(1, net.line_bits)):
        held_b = jnp.concatenate([held_b, net.in_line(held_b, 1 << bit)], 0)
    own_a = [held_a] + [net.in_plane(held_a, at) for at in range(1, places)]
    own_b = [held_b, net.in_line(held_b, 1)]
    return [own_a, [net.core(piece) for piece in own_a]], [own_b, [net.core(piece) for piece in own_b]]


def on_device(
    queries,
    kv_cache,
    lengths,
    resid,
    w_uv,
    o_proj,
    norm_gain,
    expert_ids,
    route_gates,
    expert_owner,
    gate_w,
    up_w,
    down_w,
):
    dp = lax.axis_size("dp")
    heads = lax.axis_size("heads")
    net = Net(dp, heads)
    rows_dev, width = resid.shape
    slice_width = width // heads
    tile, wide_count, narrow_count = slice_width // 14, 10, 4
    if tile % 128:
        tile, wide_count, narrow_count = slice_width // 7, 5, 2
    me = lax.axis_index("dp")
    my_head = lax.axis_index("heads")
    slots = jnp.array(
        [
            jc + 2 * jx + 4 * jz
            for jc in range(2)
            for jx in range(net.near)
            for jz in range(net.line)
        ],
        jnp.int32,
    )
    order = jnp.bitwise_xor(slots, me)
    natural = jnp.arange(dp, dtype=jnp.int32)
    cols = jnp.bitwise_xor(jnp.arange(heads, dtype=jnp.int32), my_head)

    latent_out = attend(queries, kv_cache, lengths)
    out_proj = o_proj[0].reshape(-1, width)
    gathered = lax.all_to_all(latent_out, "dp", split_axis=0, concat_axis=0, tiled=True)
    gathered = gathered.reshape(dp, -1, rows_dev, LAT)

    holder = jnp.sum(
        (expert_ids[:, :, None] == jnp.arange(expert_owner.shape[0], dtype=jnp.int32)).astype(jnp.int32)
        * expert_owner,
        -1,
    )
    table = jnp.sum(jnp.where(holder[:, :, None] == natural, route_gates[:, :, None], 0.0), 1)
    table_parts = pieces_of(table)

    resid_slice = lax.dynamic_slice_in_dim(resid, my_head * slice_width, slice_width, 1)
    gain_slice = lax.dynamic_slice_in_dim(norm_gain, my_head * slice_width, slice_width, 0)
    extra = jnp.concatenate([jnp.zeros((rows_dev, 3), BF16), *table_parts], 1)
    extra = jnp.pad(extra, ((0, 0), (0, EXTRA - extra.shape[1])))

    gain_slice = gain_slice.reshape(1, -1)
    mine = me.reshape(1).astype(jnp.int32)
    gathered, resid_slice, gain_slice, extra, order, cols, mine = lax.optimization_barrier(
        (gathered, resid_slice, gain_slice, extra, order, cols, mine)
    )
    values = values_of(gathered, w_uv[0], order)
    keep_a, send_a = project(values, out_proj, cols, None, tile, 0, wide_count)
    keep_b, send_b = project(values, out_proj, cols, None, tile, wide_count, narrow_count)
    parts_a, parts_b = reduce_both(net, (keep_a, send_a), (keep_b, send_b), rows_dev)
    mid_a, mid_b, row_a, row_b = payloads(
        parts_a, parts_b, resid_slice, gain_slice, extra
    )
    pieces_a, pieces_b = gather_both(net, row_a, row_b)

    hidden, coef, keep_a, send_a = experts_of(
        net,
        pieces_a,
        pieces_b,
        gate_w[0],
        up_w[0],
        down_w[0],
        cols,
        mine,
        tile,
        (wide_count, narrow_count),
        rows_dev,
    )
    keep_b, send_b = project(hidden, down_w[0], cols, coef, tile, wide_count, narrow_count)
    moe_a, moe_b = reduce_both(net, (keep_a, send_a), (keep_b, send_b), rows_dev)
    return jnp.concatenate(
        [mid_a + summed_with(*moe_a), mid_b + summed_with(*moe_b)], 1
    ).astype(BF16)


def solution(mesh):
    return jax.shard_map(
        on_device,
        mesh=mesh,
        in_specs=(
            P(("groups", "dp"), "heads", None),
            P(("groups", "dp"), None, None),
            P(("groups", "dp")),
            P(("groups", "dp"), None),
            P("heads", "dp", None, None),
            P("heads", "dp", None, None),
            P(),
            P(("groups", "dp"), None),
            P(("groups", "dp"), None),
            P(),
            P("dp", None, "heads"),
            P("dp", None, "heads"),
            P("dp", "heads", None),
        ),
        out_specs=P(("groups", "dp"), "heads"),
        check_vma=False,
    )
```

```python
import functools

import jax
import jax.numpy as jnp
from jax import lax
from jax.experimental import pallas as pl
from jax.experimental.pallas import tpu as pltpu
from jax.sharding import PartitionSpec as P

LAT = 512
EPSILON = 1e-06
SCORE_SCALE = 192.0 ** (-0.5)
BF16 = jnp.bfloat16
F32 = jnp.float32
EXTRA = 128
PROJECT_BYTES = 12 * 1024 * 1024
EXPERT_BYTES = 16 * 1024 * 1024
PAYLOAD_BYTES = 4 * 1024 * 1024


def attend_kernel(lengths, q_ref, cache_ref, out_ref, *scrs, rows, latent):
    heads = q_ref.shape[1]
    positions = lax.broadcasted_iota(jnp.int32, (1, cache_ref.shape[2]), 1)
    scores = [
        jnp.dot(q_ref[row], cache_ref[row], preferred_element_type=F32) * SCORE_SCALE
        for row in range(rows)
    ]
    weights = []
    for row in range(rows):
        live = positions < lengths[pl.program_id(0) * rows + row]
        score = jnp.where(live, scores[row], -jnp.inf)
        weight = jnp.exp(score - jnp.max(score, -1, keepdims=True))
        weights.append((weight / jnp.sum(weight, -1, keepdims=True)).astype(BF16))
    for row in range(rows):
        mixed = lax.dot_general(
            weights[row],
            cache_ref[row, :latent],
            (((1,), (1,)), ((), ())),
            preferred_element_type=F32,
        )
        at = (pl.program_id(0) * rows + row) * heads
        for part, scr in enumerate(scrs):
            scr[pl.ds(pl.multiple_of(at, 8), heads), :] = mixed[:, part * 128 : (part + 1) * 128]

    @pl.when(pl.program_id(0) == pl.num_programs(0) - 1)
    def _():
        for head in range(heads):
            for part, scr in enumerate(scrs):
                out_ref[head, :, part * 128 : (part + 1) * 128] = scr[
                    pl.ds(head, out_ref.shape[1], stride=heads), :
                ].astype(BF16)


def attend(queries, kv_cache, lengths):
    count, heads, depth = queries.shape
    context = kv_cache.shape[1]
    cache = jnp.swapaxes(kv_cache, 1, 2)
    rows = 8
    return pl.pallas_call(
        functools.partial(attend_kernel, rows=rows, latent=LAT),
        grid=(count // rows,),
        in_specs=[
            pl.BlockSpec(memory_space=pltpu.SMEM),
            pl.BlockSpec((rows, heads, depth), lambda i: (i, 0, 0)),
            pl.BlockSpec((rows, depth, context), lambda i: (i, 0, 0)),
        ],
        out_specs=pl.BlockSpec(memory_space=pltpu.VMEM),
        out_shape=jax.ShapeDtypeStruct((heads, count, LAT), BF16),
        scratch_shapes=[pltpu.VMEM((count * heads, 128), F32)] * (LAT // 128),
        compiler_params=pltpu.CompilerParams(vmem_limit_bytes=56 * 1024 * 1024),
    )(lengths, queries, cache)


class Net:
    def __init__(self, dp, heads):
        self.dp, self.heads = dp, heads
        self.near = 2
        self.line = dp // 4
        self.plane = [(jh, jx) for jh in range(heads) for jx in range(self.near)]
        self.line_bits = self.line.bit_length() - 1
        self.plane_bits = len(self.plane).bit_length() - 1
        slots = [0]
        for bit in reversed(range(1, self.line_bits)):
            slots = slots + [slot | 1 << bit for slot in slots]
        self.line_at = {slot | odd: (odd, at) for odd in range(2) for at, slot in enumerate(slots)}

    def move(self, value, dp_mask, heads_mask=0):
        mask = dp_mask * self.heads + heads_mask
        count = self.dp * self.heads
        return lax.ppermute(value, ("dp", "heads"), [(i, i ^ mask) for i in range(count)])

    def core(self, value):
        return self.move(value, 1)

    def in_plane(self, value, at):
        jh, jx = self.plane[at]
        return self.move(value, 2 * jx, jh)

    def in_line(self, value, jz):
        return self.move(value, 4 * jz)


def values_kernel(order, latent_ref, map_ref, out_ref, x_scr):
    sources, heads, rows, _ = latent_ref.shape
    wide = map_ref.shape[-1]
    for head in range(heads):
        for slot in range(sources):
            x_scr[slot * rows : (slot + 1) * rows, :] = latent_ref[order[slot], head]
        out = jnp.dot(x_scr[...], map_ref[head], preferred_element_type=F32)
        out_ref[:, head * wide : (head + 1) * wide] = out.astype(BF16)


def values_of(latents, maps, order):
    sources, heads, rows, latent = latents.shape
    vmem = pl.BlockSpec(memory_space=pltpu.VMEM)
    return pl.pallas_call(
        values_kernel,
        in_specs=[pl.BlockSpec(memory_space=pltpu.SMEM), vmem, vmem],
        out_specs=vmem,
        out_shape=jax.ShapeDtypeStruct((sources * rows, heads * maps.shape[-1]), BF16),
        scratch_shapes=[pltpu.VMEM((sources * rows, latent), BF16)],
        compiler_params=pltpu.CompilerParams(vmem_limit_bytes=16 * 1024 * 1024),
    )(order, latents, maps)


def put(out, keep_ref, send_ref, head, lanes):
    half = out.shape[0] // 2
    keep_ref[head, :, lanes] = out[:half].astype(BF16)
    send_ref[head, :, lanes] = out[half:].astype(BF16)


def column_lanes(cols, h, tile, first, t, slice_width):
    return pl.ds(pl.multiple_of(cols[h] * slice_width + (first + t) * tile, 128), tile)


def project_kernel(cols, *refs, tile, first, count, scaled):
    if scaled:
        x_ref, scale_ref, *refs = refs
    else:
        x_ref, *refs = refs
    w_ref, keep_ref, send_ref = refs
    heads = keep_ref.shape[0]
    slice_width = w_ref.shape[1] // heads
    for h in range(heads):
        for t in range(count):
            lanes = column_lanes(cols, h, tile, first, t, slice_width)
            out = jnp.dot(x_ref[...], w_ref[:, lanes], preferred_element_type=F32)
            if scaled:
                out = out * scale_ref[:, :1]
            put(out, keep_ref, send_ref, h, slice(t * tile, (t + 1) * tile))


def project(x, weights, cols, scale, tile, first, count):
    rows, depth = x.shape
    heads = cols.shape[0]
    out = jax.ShapeDtypeStruct((heads, rows // 2, count * tile), BF16)
    given = [x] if scale is None else [x, scale]
    vmem = pl.BlockSpec(memory_space=pltpu.VMEM)
    smem = pl.BlockSpec(memory_space=pltpu.SMEM)
    return pl.pallas_call(
        functools.partial(
            project_kernel, tile=tile, first=first, count=count, scaled=scale is not None
        ),
        in_specs=[smem] + [vmem] * (len(given) + 1),
        out_specs=[vmem, vmem],
        out_shape=[out, out],
        compiler_params=pltpu.CompilerParams(vmem_limit_bytes=PROJECT_BYTES),
        cost_estimate=pl.CostEstimate(
            flops=2 * rows * depth * count * tile * heads,
            bytes_accessed=2 * (depth + rows) * count * tile * heads,
            transcendentals=0,
        ),
    )(cols, *given, weights)


def pieces_of(value):
    high = lax.reduce_precision(value, 8, 7)
    rest = value - high
    middle = lax.reduce_precision(rest, 8, 7)
    return [high.astype(BF16), middle.astype(BF16), (rest - middle).astype(BF16)]


def row_parts(pieces, jh, net, by_line, rows_dev, lanes):
    parts = []
    for jc in range(2):
        for jx in range(net.near):
            at = jh * net.near + jx
            if by_line:
                for jz in range(net.line):
                    piece, index = net.line_at[jz]
                    start = (index * len(net.plane) + at) * rows_dev
                    parts.append(pieces[jc][piece][start : start + rows_dev, lanes])
            else:
                parts.append(pieces[jc][at][:, lanes])
    return jnp.concatenate(parts, 0)


def expert_kernel(cols, me, *refs, net, groups, rows_dev, tile, counts, down_count, width):
    pieces = []
    for per_core in groups:
        pieces.append([refs[:per_core], refs[per_core : 2 * per_core]])
        refs = refs[2 * per_core :]
    gate_ref, up_ref, down_ref, hidden_ref, coef_ref, keep_ref, send_ref, gate_acc, up_acc = refs
    heads = net.heads
    slice_width = width // heads
    plan = [
        (group, jh, t, (0 if group == 0 else counts[0]) + t)
        for group in (1, 0)
        for jh in range(heads)
        for t in range(counts[group])
    ]
    for at, (group, jh, t, in_slice) in enumerate(plan):
        x = row_parts(pieces[group], jh, net, group == 1, rows_dev, slice(t * tile, (t + 1) * tile))
        row = pl.ds(pl.multiple_of(cols[jh] * slice_width + in_slice * tile, 128), tile)
        gate = jnp.dot(x, gate_ref[row, :], preferred_element_type=F32)
        up = jnp.dot(x, up_ref[row, :], preferred_element_type=F32)
        if at == 0:
            gate_acc[...] = gate
            up_acc[...] = up
        else:
            gate_acc[...] += gate
            up_acc[...] += up

    lane = lax.broadcasted_iota(jnp.int32, (1, EXTRA), 1)
    squares = 0.0
    lanes = slice(counts[1] * tile, counts[1] * tile + EXTRA)
    for jh in range(heads):
        extra = row_parts(pieces[1], jh, net, True, rows_dev, lanes).astype(F32)
        squares = squares + extra
    squares = jnp.sum(jnp.where(lane < 3, squares, 0.0), -1, keepdims=True)
    norm = lax.rsqrt(squares / width + EPSILON)
    mine = (lane == 3 + me[0]) | (lane == 3 + net.dp + me[0]) | (lane == 3 + 2 * net.dp + me[0])
    coef = jnp.sum(jnp.where(mine, extra, 0.0), -1, keepdims=True)
    coef_ref[...] = jnp.broadcast_to(coef, coef_ref.shape)
    gate = gate_acc[...] * norm
    up = up_acc[...] * norm
    hidden_ref[...] = (gate / (1.0 + jnp.exp(-gate)) * up).astype(BF16)
    for h in range(heads):
        for t in range(down_count):
            lanes = column_lanes(cols, h, tile, 0, t, slice_width)
            out = jnp.dot(hidden_ref[...], down_ref[:, lanes], preferred_element_type=F32) * coef
            put(out, keep_ref, send_ref, h, slice(t * tile, (t + 1) * tile))


def experts_of(net, pieces_a, pieces_b, gate_w, up_w, down_w, cols, me, tile, counts, down_count, rows_dev):
    flat = [piece for pieces in (pieces_a, pieces_b) for group in pieces for piece in group]
    width, hidden = gate_w.shape
    rows = net.dp * rows_dev
    heads = net.heads
    vmem = pl.BlockSpec(memory_space=pltpu.VMEM)
    smem = pl.BlockSpec(memory_space=pltpu.SMEM)
    out = jax.ShapeDtypeStruct((heads, rows // 2, down_count * tile), BF16)
    return pl.pallas_call(
        functools.partial(
            expert_kernel,
            net=net,
            groups=(len(pieces_a[0]), len(pieces_b[0])),
            rows_dev=rows_dev,
            tile=tile,
            counts=counts,
            down_count=down_count,
            width=width,
        ),
        in_specs=[smem, smem] + [vmem] * (len(flat) + 3),
        out_specs=[vmem] * 4,
        out_shape=[
            jax.ShapeDtypeStruct((rows, hidden), BF16),
            jax.ShapeDtypeStruct((rows, EXTRA), F32),
            out,
            out,
        ],
        scratch_shapes=[
            pltpu.VMEM((rows, hidden), F32),
            pltpu.VMEM((rows, hidden), F32),
        ],
        compiler_params=pltpu.CompilerParams(vmem_limit_bytes=EXPERT_BYTES),
        cost_estimate=pl.CostEstimate(
            flops=6 * rows * width * hidden,
            bytes_accessed=6 * width * hidden,
            transcendentals=0,
        ),
    )(cols, me, *flat, gate_w, up_w, down_w)


def payload_kernel(*refs, arrived, split):
    own, rest = refs[:2], refs[2:]
    received, rest = [rest[: arrived[0]], rest[arrived[0] : sum(arrived)]], rest[sum(arrived) :]
    resid_ref, gain_ref, extra_ref = rest[:3]
    mids, rows = rest[3:5], rest[5:7]
    lane = lax.broadcasted_iota(jnp.int32, (1, EXTRA), 1)
    start = 0
    squares = 0.0
    for which in range(2):
        total = own[which][...]
        for ref in received[which]:
            total = total + ref[...].astype(F32)
        size = total.shape[-1]
        mid = resid_ref[:, start : start + size].astype(F32) + total
        mids[which][...] = mid
        row = (mid * gain_ref[:, start : start + size].astype(F32)).astype(BF16)
        if which == 0:
            rows[0][:, :size] = row
        else:
            more = split - start
            rows[0][:, start:split] = row[:, :more]
            rows[1][:, : size - more] = row[:, more:]
        squares = squares + jnp.sum(mid * mid, -1, keepdims=True)
        start += size
    high = squares.astype(BF16)
    left = squares - high.astype(F32)
    middle = left.astype(BF16)
    low = (left - middle.astype(F32)).astype(BF16)
    extra = extra_ref[...]
    for at, part in enumerate((high, middle, low)):
        extra = jnp.where(lane == at, jnp.broadcast_to(part, extra.shape), extra)
    rows[1][:, start - split :] = extra


def payloads(parts_a, parts_b, resid, gain, extra, split):
    own_a, in_a = parts_a
    own_b, in_b = parts_b
    rows = own_a.shape[0]
    mids = [jax.ShapeDtypeStruct(own.shape, F32) for own in (own_a, own_b)]
    outs = [
        jax.ShapeDtypeStruct((rows, split), BF16),
        jax.ShapeDtypeStruct((rows, resid.shape[1] - split + EXTRA), BF16),
    ]
    operands = [own_a, own_b, *in_a, *in_b, resid, gain, extra]
    vmem = pl.BlockSpec(memory_space=pltpu.VMEM)
    return pl.pallas_call(
        functools.partial(
            payload_kernel, arrived=(len(in_a), len(in_b)), split=split
        ),
        in_specs=[vmem] * len(operands),
        out_specs=[vmem] * 4,
        out_shape=mids + outs,
        compiler_params=pltpu.CompilerParams(vmem_limit_bytes=PAYLOAD_BYTES),
    )(*operands)


def summed_with(own, arrived):
    for value in arrived:
        own = own + value.astype(F32)
    return own


def reduce_both(net, first, second, rows_dev):
    places, line = len(net.plane), net.line
    (keep_a, send_a), (keep_b, send_b) = first, second
    other_a, other_b = net.core(send_a), net.core(send_b)
    shape_a = (places, line * rows_dev, keep_a.shape[-1])
    shape_b = (places, line, rows_dev, keep_b.shape[-1])
    keep_a, other_a = keep_a.reshape(shape_a), other_a.reshape(shape_a)
    keep_b, other_b = keep_b.reshape(shape_b), other_b.reshape(shape_b)
    sum_a = [keep_a[at].astype(F32) + other_a[at].astype(F32) for at in range(places)]
    sum_b = {jz: keep_b[:, jz].astype(F32) + other_b[:, jz].astype(F32) for jz in range(line)}
    go_a = [value.astype(BF16) for value in sum_a[1:]]
    go_b = [sum_b[jz].astype(BF16) for jz in range(1, line)]
    go_a, go_b = lax.optimization_barrier((go_a, go_b))
    in_b = [net.in_line(value, jz + 1) for jz, value in enumerate(go_b)]
    in_a = [net.in_plane(value, at + 1) for at, value in enumerate(go_a)]
    sum_a = summed_with(sum_a[0], in_a).reshape(line, rows_dev, keep_a.shape[-1])
    sum_a, in_b = lax.optimization_barrier((sum_a, in_b))
    sum_b = summed_with(sum_b[0], in_b)
    go_a = [sum_a[jz].astype(BF16) for jz in range(1, line)]
    sum_b = {at: sum_b[at] for at in range(places)}
    go_b, sum_b = split_pairs(sum_b, 0)
    go_a, go_b = lax.optimization_barrier((go_a, go_b))
    for bit in range(net.plane_bits):
        if bit:
            go_b, sum_b = split_pairs(sum_b, bit)
        last = net.in_plane(go_b, 1 << bit)
        if bit < net.plane_bits - 1:
            sum_b = join_pairs(sum_b, last)
    in_a = [net.in_line(value, jz + 1) for jz, value in enumerate(go_a)]
    return (sum_a[0], in_a), (sum_b[0], [last.reshape(rows_dev, -1)])


def split_pairs(parts, bit):
    go = jnp.stack([parts[slot].astype(BF16) for slot in sorted(parts) if slot >> bit & 1])
    return go, {slot: value for slot, value in parts.items() if not slot >> bit & 1}


def join_pairs(parts, arrived):
    return {slot: parts[slot] + arrived[at].astype(F32) for at, slot in enumerate(sorted(parts))}


def gather_both(net, row_a, row_b):
    places, line = len(net.plane), net.line
    row_a, row_b = lax.optimization_barrier((row_a, row_b))
    in_a = [net.in_line(row_a, jz) for jz in range(1, line)]
    held_a = jnp.concatenate([row_a] + in_a, 0)
    held_b = row_b
    for bit in range(net.plane_bits):
        last = net.in_plane(held_b, 1 << bit)
        if bit == net.plane_bits - 1:
            held_a, last = lax.optimization_barrier((held_a, last))
        held_b = jnp.concatenate([held_b, last], 0)
    held_a, held_b = lax.optimization_barrier((held_a, held_b))
    for bit in reversed(range(1, net.line_bits)):
        held_b = jnp.concatenate([held_b, net.in_line(held_b, 1 << bit)], 0)
    own_a = [held_a] + [net.in_plane(held_a, at) for at in range(1, places)]
    own_b = [held_b, net.in_line(held_b, 1)]
    return [own_a, [net.core(piece) for piece in own_a]], [own_b, [net.core(piece) for piece in own_b]]


def on_device(
    queries,
    kv_cache,
    lengths,
    resid,
    w_uv,
    o_proj,
    norm_gain,
    expert_ids,
    route_gates,
    expert_owner,
    gate_w,
    up_w,
    down_w,
):
    dp = lax.axis_size("dp")
    heads = lax.axis_size("heads")
    net = Net(dp, heads)
    rows_dev, width = resid.shape
    slice_width = width // heads
    tile, wide_count, narrow_count = slice_width // 14, 10, 4
    if tile % 128:
        tile, wide_count, narrow_count = slice_width // 7, 5, 2
    gather_counts = (wide_count + 1, narrow_count - 1)
    me = lax.axis_index("dp")
    my_head = lax.axis_index("heads")
    slots = jnp.array(
        [
            jc + 2 * jx + 4 * jz
            for jc in range(2)
            for jx in range(net.near)
            for jz in range(net.line)
        ],
        jnp.int32,
    )
    order = jnp.bitwise_xor(slots, me)
    natural = jnp.arange(dp, dtype=jnp.int32)
    cols = jnp.bitwise_xor(jnp.arange(heads, dtype=jnp.int32), my_head)

    latent_out = attend(queries, kv_cache, lengths)
    out_proj = o_proj[0].reshape(-1, width)
    gathered = lax.all_to_all(latent_out, "dp", split_axis=0, concat_axis=0, tiled=True)
    gathered = gathered.reshape(dp, -1, rows_dev, LAT)

    holder = jnp.sum(
        (expert_ids[:, :, None] == jnp.arange(expert_owner.shape[0], dtype=jnp.int32)).astype(jnp.int32)
        * expert_owner,
        -1,
    )
    table = jnp.sum(jnp.where(holder[:, :, None] == natural, route_gates[:, :, None], 0.0), 1)
    table_parts = pieces_of(table)

    resid_slice = lax.dynamic_slice_in_dim(resid, my_head * slice_width, slice_width, 1)
    gain_slice = lax.dynamic_slice_in_dim(norm_gain, my_head * slice_width, slice_width, 0)
    extra = jnp.concatenate([jnp.zeros((rows_dev, 3), BF16), *table_parts], 1)
    extra = jnp.pad(extra, ((0, 0), (0, EXTRA - extra.shape[1])))

    gain_slice = gain_slice.reshape(1, -1)
    mine = me.reshape(1).astype(jnp.int32)
    gathered, resid_slice, gain_slice, extra, order, cols, mine = lax.optimization_barrier(
        (gathered, resid_slice, gain_slice, extra, order, cols, mine)
    )
    values = values_of(gathered, w_uv[0], order)
    keep_a, send_a = project(values, out_proj, cols, None, tile, 0, wide_count)
    keep_b, send_b = project(values, out_proj, cols, None, tile, wide_count, narrow_count)
    parts_a, parts_b = reduce_both(net, (keep_a, send_a), (keep_b, send_b), rows_dev)
    mid_a, mid_b, row_a, row_b = payloads(
        parts_a, parts_b, resid_slice, gain_slice, extra, gather_counts[0] * tile
    )
    pieces_a, pieces_b = gather_both(net, row_a, row_b)

    hidden, coef, keep_a, send_a = experts_of(
        net,
        pieces_a,
        pieces_b,
        gate_w[0],
        up_w[0],
        down_w[0],
        cols,
        mine,
        tile,
        gather_counts,
        wide_count,
        rows_dev,
    )
    keep_b, send_b = project(hidden, down_w[0], cols, coef, tile, wide_count, narrow_count)
    moe_a, moe_b = reduce_both(net, (keep_a, send_a), (keep_b, send_b), rows_dev)
    return jnp.concatenate(
        [mid_a + summed_with(*moe_a), mid_b + summed_with(*moe_b)], 1
    ).astype(BF16)


def solution(mesh):
    return jax.shard_map(
        on_device,
        mesh=mesh,
        in_specs=(
            P(("groups", "dp"), "heads", None),
            P(("groups", "dp"), None, None),
            P(("groups", "dp")),
            P(("groups", "dp"), None),
            P("heads", "dp", None, None),
            P("heads", "dp", None, None),
            P(),
            P(("groups", "dp"), None),
            P(("groups", "dp"), None),
            P(),
            P("dp", None, "heads"),
            P("dp", None, "heads"),
            P("dp", "heads", None),
        ),
        out_specs=P(("groups", "dp"), "heads"),
        check_vma=False,
    )
```

```python
import functools

import jax
import jax.numpy as jnp
from jax import lax
from jax.experimental import pallas as pl
from jax.experimental.pallas import tpu as pltpu
from jax.sharding import PartitionSpec as P

LAT = 512
EPSILON = 1e-06
SCORE_SCALE = 192.0 ** (-0.5)
BF16 = jnp.bfloat16
F32 = jnp.float32
EXTRA = 128
PROJECT_BYTES = 12 * 1024 * 1024
EXPERT_BYTES = 16 * 1024 * 1024
PAYLOAD_BYTES = 4 * 1024 * 1024


def attend_kernel(lengths, q_ref, cache_ref, out_ref, *scrs, rows, latent):
    heads = q_ref.shape[1]
    positions = lax.broadcasted_iota(jnp.int32, (1, cache_ref.shape[2]), 1)
    scores = [
        jnp.dot(q_ref[row], cache_ref[row], preferred_element_type=F32) * SCORE_SCALE
        for row in range(rows)
    ]
    weights = []
    for row in range(rows):
        live = positions < lengths[pl.program_id(0) * rows + row]
        score = jnp.where(live, scores[row], -jnp.inf)
        weight = jnp.exp(score - jnp.max(score, -1, keepdims=True))
        weights.append((weight / jnp.sum(weight, -1, keepdims=True)).astype(BF16))
    for row in range(rows):
        mixed = lax.dot_general(
            weights[row],
            cache_ref[row, :latent],
            (((1,), (1,)), ((), ())),
            preferred_element_type=F32,
        )
        at = (pl.program_id(0) * rows + row) * heads
        for part, scr in enumerate(scrs):
            scr[pl.ds(pl.multiple_of(at, 8), heads), :] = mixed[:, part * 128 : (part + 1) * 128]

    @pl.when(pl.program_id(0) == pl.num_programs(0) - 1)
    def _():
        for head in range(heads):
            for part, scr in enumerate(scrs):
                out_ref[head, :, part * 128 : (part + 1) * 128] = scr[
                    pl.ds(head, out_ref.shape[1], stride=heads), :
                ].astype(BF16)


def attend(queries, kv_cache, lengths):
    count, heads, depth = queries.shape
    context = kv_cache.shape[1]
    cache = jnp.swapaxes(kv_cache, 1, 2)
    rows = 8
    return pl.pallas_call(
        functools.partial(attend_kernel, rows=rows, latent=LAT),
        grid=(count // rows,),
        in_specs=[
            pl.BlockSpec(memory_space=pltpu.SMEM),
            pl.BlockSpec((rows, heads, depth), lambda i: (i, 0, 0)),
            pl.BlockSpec((rows, depth, context), lambda i: (i, 0, 0)),
        ],
        out_specs=pl.BlockSpec(memory_space=pltpu.VMEM),
        out_shape=jax.ShapeDtypeStruct((heads, count, LAT), BF16),
        scratch_shapes=[pltpu.VMEM((count * heads, 128), F32)] * (LAT // 128),
        compiler_params=pltpu.CompilerParams(vmem_limit_bytes=56 * 1024 * 1024),
    )(lengths, queries, cache)


class Net:
    def __init__(self, dp, heads):
        self.dp, self.heads = dp, heads
        self.near = 2
        self.line = dp // 4
        self.plane = [(jh, jx) for jh in range(heads) for jx in range(self.near)]
        self.line_bits = self.line.bit_length() - 1
        self.plane_bits = len(self.plane).bit_length() - 1
        slots = [0]
        for bit in reversed(range(1, self.line_bits)):
            slots = slots + [slot | 1 << bit for slot in slots]
        self.line_at = {slot | odd: (odd, at) for odd in range(2) for at, slot in enumerate(slots)}

    def move(self, value, dp_mask, heads_mask=0):
        mask = dp_mask * self.heads + heads_mask
        count = self.dp * self.heads
        return lax.ppermute(value, ("dp", "heads"), [(i, i ^ mask) for i in range(count)])

    def core(self, value):
        return self.move(value, 1)

    def in_plane(self, value, at):
        jh, jx = self.plane[at]
        return self.move(value, 2 * jx, jh)

    def in_line(self, value, jz):
        return self.move(value, 4 * jz)


def values_kernel(order, latent_ref, map_ref, out_ref, x_scr):
    sources, heads, rows, _ = latent_ref.shape
    wide = map_ref.shape[-1]
    for head in range(heads):
        for slot in range(sources):
            x_scr[slot * rows : (slot + 1) * rows, :] = latent_ref[order[slot], head]
        out = jnp.dot(x_scr[...], map_ref[head], preferred_element_type=F32)
        out_ref[:, head * wide : (head + 1) * wide] = out.astype(BF16)


def values_of(latents, maps, order):
    sources, heads, rows, latent = latents.shape
    vmem = pl.BlockSpec(memory_space=pltpu.VMEM)
    return pl.pallas_call(
        values_kernel,
        in_specs=[pl.BlockSpec(memory_space=pltpu.SMEM), vmem, vmem],
        out_specs=vmem,
        out_shape=jax.ShapeDtypeStruct((sources * rows, heads * maps.shape[-1]), BF16),
        scratch_shapes=[pltpu.VMEM((sources * rows, latent), BF16)],
        compiler_params=pltpu.CompilerParams(vmem_limit_bytes=16 * 1024 * 1024),
    )(order, latents, maps)


def put(out, keep_ref, send_ref, head, lanes):
    half = out.shape[0] // 2
    keep_ref[head, :, lanes] = out[:half].astype(BF16)
    send_ref[head, :, lanes] = out[half:].astype(BF16)


def column_lanes(cols, h, tile, first, t, slice_width):
    return pl.ds(pl.multiple_of(cols[h] * slice_width + (first + t) * tile, 128), tile)


def project_kernel(cols, *refs, tile, first, count, scaled):
    if scaled:
        x_ref, scale_ref, *refs = refs
    else:
        x_ref, *refs = refs
    w_ref, keep_ref, send_ref = refs
    heads = keep_ref.shape[0]
    slice_width = w_ref.shape[1] // heads
    for h in range(heads):
        for t in range(count):
            lanes = column_lanes(cols, h, tile, first, t, slice_width)
            out = jnp.dot(x_ref[...], w_ref[:, lanes], preferred_element_type=F32)
            if scaled:
                out = out * scale_ref[:, :1]
            put(out, keep_ref, send_ref, h, slice(t * tile, (t + 1) * tile))


def project(x, weights, cols, scale, tile, first, count):
    rows, depth = x.shape
    heads = cols.shape[0]
    out = jax.ShapeDtypeStruct((heads, rows // 2, count * tile), BF16)
    given = [x] if scale is None else [x, scale]
    vmem = pl.BlockSpec(memory_space=pltpu.VMEM)
    smem = pl.BlockSpec(memory_space=pltpu.SMEM)
    return pl.pallas_call(
        functools.partial(
            project_kernel, tile=tile, first=first, count=count, scaled=scale is not None
        ),
        in_specs=[smem] + [vmem] * (len(given) + 1),
        out_specs=[vmem, vmem],
        out_shape=[out, out],
        compiler_params=pltpu.CompilerParams(vmem_limit_bytes=PROJECT_BYTES),
        cost_estimate=pl.CostEstimate(
            flops=2 * rows * depth * count * tile * heads,
            bytes_accessed=2 * (depth + rows) * count * tile * heads,
            transcendentals=0,
        ),
    )(cols, *given, weights)


def pieces_of(value):
    high = lax.reduce_precision(value, 8, 7)
    rest = value - high
    middle = lax.reduce_precision(rest, 8, 7)
    return [high.astype(BF16), middle.astype(BF16), (rest - middle).astype(BF16)]


def row_parts(pieces, jh, net, by_line, rows_dev, lanes):
    parts = []
    for jc in range(2):
        for jx in range(net.near):
            at = jh * net.near + jx
            if by_line:
                for jz in range(net.line):
                    piece, index = net.line_at[jz]
                    start = (index * len(net.plane) + at) * rows_dev
                    parts.append(pieces[jc][piece][start : start + rows_dev, lanes])
            else:
                parts.append(pieces[jc][at][:, lanes])
    return jnp.concatenate(parts, 0)


def expert_kernel(cols, me, *refs, net, groups, rows_dev, tile, counts, down_count, width):
    pieces = []
    for per_core in groups:
        pieces.append([refs[:per_core], refs[per_core : 2 * per_core]])
        refs = refs[2 * per_core :]
    gate_ref, up_ref, down_ref, hidden_ref, coef_ref, keep_ref, send_ref, gate_acc, up_acc = refs
    heads = net.heads
    slice_width = width // heads
    plan = [
        (group, jh, t, (0 if group == 0 else counts[0]) + t)
        for group in (1, 0)
        for jh in range(heads)
        for t in range(counts[group])
    ]
    for at, (group, jh, t, in_slice) in enumerate(plan):
        x = row_parts(pieces[group], jh, net, group == 1, rows_dev, slice(t * tile, (t + 1) * tile))
        row = pl.ds(pl.multiple_of(cols[jh] * slice_width + in_slice * tile, 128), tile)
        gate = jnp.dot(x, gate_ref[row, :], preferred_element_type=F32)
        up = jnp.dot(x, up_ref[row, :], preferred_element_type=F32)
        if at == 0:
            gate_acc[...] = gate
            up_acc[...] = up
        else:
            gate_acc[...] += gate
            up_acc[...] += up

    lane = lax.broadcasted_iota(jnp.int32, (1, EXTRA), 1)
    squares = 0.0
    lanes = slice(counts[1] * tile, counts[1] * tile + EXTRA)
    for jh in range(heads):
        extra = row_parts(pieces[1], jh, net, True, rows_dev, lanes).astype(F32)
        squares = squares + extra
    squares = jnp.sum(jnp.where(lane < 3, squares, 0.0), -1, keepdims=True)
    norm = lax.rsqrt(squares / width + EPSILON)
    mine = (lane == 3 + me[0]) | (lane == 3 + net.dp + me[0]) | (lane == 3 + 2 * net.dp + me[0])
    coef = jnp.sum(jnp.where(mine, extra, 0.0), -1, keepdims=True)
    coef_ref[...] = jnp.broadcast_to(coef, coef_ref.shape)
    gate = gate_acc[...] * norm
    up = up_acc[...] * norm
    hidden_ref[...] = (gate / (1.0 + jnp.exp(-gate)) * up).astype(BF16)
    for h in range(heads):
        for t in range(down_count):
            lanes = column_lanes(cols, h, tile, 0, t, slice_width)
            out = jnp.dot(hidden_ref[...], down_ref[:, lanes], preferred_element_type=F32) * coef
            put(out, keep_ref, send_ref, h, slice(t * tile, (t + 1) * tile))


def experts_of(net, pieces_a, pieces_b, gate_w, up_w, down_w, cols, me, tile, counts, down_count, rows_dev):
    flat = [piece for pieces in (pieces_a, pieces_b) for group in pieces for piece in group]
    width, hidden = gate_w.shape
    rows = net.dp * rows_dev
    heads = net.heads
    vmem = pl.BlockSpec(memory_space=pltpu.VMEM)
    smem = pl.BlockSpec(memory_space=pltpu.SMEM)
    out = jax.ShapeDtypeStruct((heads, rows // 2, down_count * tile), BF16)
    return pl.pallas_call(
        functools.partial(
            expert_kernel,
            net=net,
            groups=(len(pieces_a[0]), len(pieces_b[0])),
            rows_dev=rows_dev,
            tile=tile,
            counts=counts,
            down_count=down_count,
            width=width,
        ),
        in_specs=[smem, smem] + [vmem] * (len(flat) + 3),
        out_specs=[vmem] * 4,
        out_shape=[
            jax.ShapeDtypeStruct((rows, hidden), BF16),
            jax.ShapeDtypeStruct((rows, EXTRA), F32),
            out,
            out,
        ],
        scratch_shapes=[
            pltpu.VMEM((rows, hidden), F32),
            pltpu.VMEM((rows, hidden), F32),
        ],
        compiler_params=pltpu.CompilerParams(vmem_limit_bytes=EXPERT_BYTES),
        cost_estimate=pl.CostEstimate(
            flops=6 * rows * width * hidden,
            bytes_accessed=6 * width * hidden,
            transcendentals=0,
        ),
    )(cols, me, *flat, gate_w, up_w, down_w)


def payload_kernel(*refs, arrived, split):
    own, rest = refs[:2], refs[2:]
    received, rest = [rest[: arrived[0]], rest[arrived[0] : sum(arrived)]], rest[sum(arrived) :]
    resid_ref, gain_ref, extra_ref = rest[:3]
    mids, rows = rest[3:5], rest[5:7]
    lane = lax.broadcasted_iota(jnp.int32, (1, EXTRA), 1)
    start = 0
    squares = 0.0
    for which in range(2):
        total = own[which][...]
        for ref in received[which]:
            total = total + ref[...].astype(F32)
        size = total.shape[-1]
        mid = resid_ref[:, start : start + size].astype(F32) + total
        mids[which][...] = mid
        row = (mid * gain_ref[:, start : start + size].astype(F32)).astype(BF16)
        if which == 0:
            rows[0][:, :size] = row
        else:
            more = split - start
            rows[0][:, start:split] = row[:, :more]
            rows[1][:, : size - more] = row[:, more:]
        squares = squares + jnp.sum(mid * mid, -1, keepdims=True)
        start += size
    high = squares.astype(BF16)
    left = squares - high.astype(F32)
    middle = left.astype(BF16)
    low = (left - middle.astype(F32)).astype(BF16)
    extra = extra_ref[...]
    for at, part in enumerate((high, middle, low)):
        extra = jnp.where(lane == at, jnp.broadcast_to(part, extra.shape), extra)
    rows[1][:, start - split :] = extra


def payloads(parts_a, parts_b, resid, gain, extra, split):
    own_a, in_a = parts_a
    own_b, in_b = parts_b
    rows = own_a.shape[0]
    mids = [jax.ShapeDtypeStruct(own.shape, F32) for own in (own_a, own_b)]
    outs = [
        jax.ShapeDtypeStruct((rows, split), BF16),
        jax.ShapeDtypeStruct((rows, resid.shape[1] - split + EXTRA), BF16),
    ]
    operands = [own_a, own_b, *in_a, *in_b, resid, gain, extra]
    vmem = pl.BlockSpec(memory_space=pltpu.VMEM)
    return pl.pallas_call(
        functools.partial(
            payload_kernel, arrived=(len(in_a), len(in_b)), split=split
        ),
        in_specs=[vmem] * len(operands),
        out_specs=[vmem] * 4,
        out_shape=mids + outs,
        compiler_params=pltpu.CompilerParams(vmem_limit_bytes=PAYLOAD_BYTES),
    )(*operands)


def summed_with(own, arrived):
    for value in arrived:
        own = own + value.astype(F32)
    return own


def reduce_both(net, first, second, rows_dev):
    places, line = len(net.plane), net.line
    (keep_a, send_a), (keep_b, send_b) = first, second
    other_a, other_b = net.core(send_a), net.core(send_b)
    shape_a = (places, line * rows_dev, keep_a.shape[-1])
    shape_b = (places, line, rows_dev, keep_b.shape[-1])
    keep_a, other_a = keep_a.reshape(shape_a), other_a.reshape(shape_a)
    keep_b, other_b = keep_b.reshape(shape_b), other_b.reshape(shape_b)
    sum_a = [keep_a[at].astype(F32) + other_a[at].astype(F32) for at in range(places)]
    sum_b = {jz: keep_b[:, jz].astype(F32) + other_b[:, jz].astype(F32) for jz in range(line)}
    go_a = [value.astype(BF16) for value in sum_a[1:]]
    go_b = [sum_b[jz].astype(BF16) for jz in range(1, line)]
    go_a, go_b = lax.optimization_barrier((go_a, go_b))
    in_b = [net.in_line(value, jz + 1) for jz, value in enumerate(go_b)]
    in_a = [net.in_plane(value, at + 1) for at, value in enumerate(go_a)]
    sum_a = summed_with(sum_a[0], in_a).reshape(line, rows_dev, keep_a.shape[-1])
    sum_a, in_b = lax.optimization_barrier((sum_a, in_b))
    sum_b = summed_with(sum_b[0], in_b)
    go_a = [sum_a[jz].astype(BF16) for jz in range(1, line)]
    sum_b = {at: sum_b[at] for at in range(places)}
    go_b, sum_b = split_pairs(sum_b, 0)
    go_a, go_b = lax.optimization_barrier((go_a, go_b))
    for bit in range(net.plane_bits):
        if bit:
            go_b, sum_b = split_pairs(sum_b, bit)
        last = net.in_plane(go_b, 1 << bit)
        if bit < net.plane_bits - 1:
            sum_b = join_pairs(sum_b, last)
    in_a = [net.in_line(value, jz + 1) for jz, value in enumerate(go_a)]
    return (sum_a[0], in_a), (sum_b[0], [last.reshape(rows_dev, -1)])


def split_pairs(parts, bit):
    go = jnp.stack([parts[slot].astype(BF16) for slot in sorted(parts) if slot >> bit & 1])
    return go, {slot: value for slot, value in parts.items() if not slot >> bit & 1}


def join_pairs(parts, arrived):
    return {slot: parts[slot] + arrived[at].astype(F32) for at, slot in enumerate(sorted(parts))}


def gather_both(net, row_a, row_b):
    places, line = len(net.plane), net.line
    row_a, row_b = lax.optimization_barrier((row_a, row_b))
    in_a = [net.in_line(row_a, jz) for jz in range(1, line)]
    held_a = jnp.concatenate([row_a] + in_a, 0)
    held_b = row_b
    for bit in range(net.plane_bits):
        last = net.in_plane(held_b, 1 << bit)
        if bit == net.plane_bits - 1:
            held_a, last = lax.optimization_barrier((held_a, last))
        held_b = jnp.concatenate([held_b, last], 0)
    for bit in reversed(range(1, net.line_bits)):
        held_b = jnp.concatenate([held_b, net.in_line(held_b, 1 << bit)], 0)
    own_a = [held_a] + [net.in_plane(held_a, at) for at in range(1, places)]
    own_b = [held_b, net.in_line(held_b, 1)]
    return [own_a, [net.core(piece) for piece in own_a]], [own_b, [net.core(piece) for piece in own_b]]


def on_device(
    queries,
    kv_cache,
    lengths,
    resid,
    w_uv,
    o_proj,
    norm_gain,
    expert_ids,
    route_gates,
    expert_owner,
    gate_w,
    up_w,
    down_w,
):
    dp = lax.axis_size("dp")
    heads = lax.axis_size("heads")
    net = Net(dp, heads)
    rows_dev, width = resid.shape
    slice_width = width // heads
    tile, wide_count, narrow_count = slice_width // 14, 10, 4
    if tile % 128:
        tile, wide_count, narrow_count = slice_width // 7, 5, 2
    gather_counts = (wide_count + 1, narrow_count - 1)
    me = lax.axis_index("dp")
    my_head = lax.axis_index("heads")
    slots = jnp.array(
        [
            jc + 2 * jx + 4 * jz
            for jc in range(2)
            for jx in range(net.near)
            for jz in range(net.line)
        ],
        jnp.int32,
    )
    order = jnp.bitwise_xor(slots, me)
    natural = jnp.arange(dp, dtype=jnp.int32)
    cols = jnp.bitwise_xor(jnp.arange(heads, dtype=jnp.int32), my_head)

    latent_out = attend(queries, kv_cache, lengths)
    out_proj = o_proj[0].reshape(-1, width)
    gathered = lax.all_to_all(latent_out, "dp", split_axis=0, concat_axis=0, tiled=True)
    gathered = gathered.reshape(dp, -1, rows_dev, LAT)

    holder = jnp.sum(
        (expert_ids[:, :, None] == jnp.arange(expert_owner.shape[0], dtype=jnp.int32)).astype(jnp.int32)
        * expert_owner,
        -1,
    )
    table = jnp.sum(jnp.where(holder[:, :, None] == natural, route_gates[:, :, None], 0.0), 1)
    table_parts = pieces_of(table)

    resid_slice = lax.dynamic_slice_in_dim(resid, my_head * slice_width, slice_width, 1)
    gain_slice = lax.dynamic_slice_in_dim(norm_gain, my_head * slice_width, slice_width, 0)
    extra = jnp.concatenate([jnp.zeros((rows_dev, 3), BF16), *table_parts], 1)
    extra = jnp.pad(extra, ((0, 0), (0, EXTRA - extra.shape[1])))

    gain_slice = gain_slice.reshape(1, -1)
    mine = me.reshape(1).astype(jnp.int32)
    gathered, resid_slice, gain_slice, extra, order, cols, mine = lax.optimization_barrier(
        (gathered, resid_slice, gain_slice, extra, order, cols, mine)
    )
    values = values_of(gathered, w_uv[0], order)
    keep_a, send_a = project(values, out_proj, cols, None, tile, 0, wide_count)
    keep_b, send_b = project(values, out_proj, cols, None, tile, wide_count, narrow_count)
    parts_a, parts_b = reduce_both(net, (keep_a, send_a), (keep_b, send_b), rows_dev)
    mid_a, mid_b, row_a, row_b = payloads(
        parts_a, parts_b, resid_slice, gain_slice, extra, gather_counts[0] * tile
    )
    pieces_a, pieces_b = gather_both(net, row_a, row_b)

    hidden, coef, keep_a, send_a = experts_of(
        net,
        pieces_a,
        pieces_b,
        gate_w[0],
        up_w[0],
        down_w[0],
        cols,
        mine,
        tile,
        gather_counts,
        wide_count,
        rows_dev,
    )
    keep_b, send_b = project(hidden, down_w[0], cols, coef, tile, wide_count, narrow_count)
    moe_a, moe_b = reduce_both(net, (keep_a, send_a), (keep_b, send_b), rows_dev)
    return jnp.concatenate(
        [mid_a + summed_with(*moe_a), mid_b + summed_with(*moe_b)], 1
    ).astype(BF16)


def solution(mesh):
    return jax.shard_map(
        on_device,
        mesh=mesh,
        in_specs=(
            P(("groups", "dp"), "heads", None),
            P(("groups", "dp"), None, None),
            P(("groups", "dp")),
            P(("groups", "dp"), None),
            P("heads", "dp", None, None),
            P("heads", "dp", None, None),
            P(),
            P(("groups", "dp"), None),
            P(("groups", "dp"), None),
            P(),
            P("dp", None, "heads"),
            P("dp", None, "heads"),
            P("dp", "heads", None),
        ),
        out_specs=P(("groups", "dp"), "heads"),
        check_vma=False,
    )
```
